256 devices in a mesh: row: 8 (over y, x_lo), col: 32 (over x_hi, z, core).
Axes of the slice: x: 4 (x_hi: 2, x_lo: 2; x = x_hi * 2 + x_lo), y: 4, z: 8, core: 2. Of those that a mesh axis runs over, the one named last changes fastest.
Arguments:
- features: bfloat16 [131072, 256], P(('row', 'col')), may hold values from -6 to 6
- weight: bfloat16 [256, 256], replicated, may hold values from -0.375 to 0.375
- cotangent: bfloat16 [131072, 256], P(('row', 'col')), may hold values from -6 to 6
- tile_rows: int32 [8, 32, 128], P('row', 'col'), may hold values from 0 to 127, as said below
- tile_cols: int32 [8, 32, 128], P('row', 'col'), may hold values from 0 to 31
- tile_values: bfloat16 [8, 32, 128, 128, 128], P('row', 'col'), may hold values from -0.09375 to 0.09375
- tile_count: int32 [8, 32], P('row', 'col'), may hold values from 32 to 128, as said below
Outputs:
- hidden: bfloat16 [131072, 256], P(('row', 'col'))
- grad_feat: bfloat16 [131072, 256], P(('row', 'col'))
- grad_weight: float32 [256, 256], replicated
The draws below stay inside these ranges and needn't reach their ends.
Inputs may be any that keep to these rules, and one draw needn't show every extreme that they name: `tile_rows`: within one grid position the slots name distinct pairs of block row and block column. `tile_count`: some grid position uses all 128 slots and some uses 128 // 4.
All inputs are finite; a program needn't handle non-finite values.
Results may differ from the reference program's by a relative error of at most 0.018.
Values may be sent and summed in bfloat16 or wider, within the bound.
A program may use at most 192 MiB of HBM per device.

```python
import jax
import jax.numpy as jnp
from jax import lax

TILE = 128
FEAT = 256
BLK_DEV = 4
ROW_GROUPS = 8
COL_GROUPS = 32
ROW_BLOCKS = 128
COL_BLOCKS = 32
TILES_DEV = 128
NODES = 131072


def tile_slots(key):
    keys = jax.random.split(key, ROW_GROUPS * COL_GROUPS)
    chosen = jax.vmap(lambda single: jax.random.permutation(single, ROW_BLOCKS * COL_BLOCKS)[:TILES_DEV])(keys)
    return chosen.reshape(ROW_GROUPS, COL_GROUPS, TILES_DEV).astype(jnp.int32)


def draw_tile_rows(key, part):
    chosen = tile_slots(key)
    return (chosen // COL_BLOCKS).astype(jnp.int32)


def draw_tile_cols(key, part):
    chosen = tile_slots(key)
    return (chosen % COL_BLOCKS).astype(jnp.int32)


def draw_tile_count(key, part):
    key = jax.random.fold_in(key, 3)
    grid = ROW_GROUPS * COL_GROUPS
    counts = jax.random.randint(key, (grid,), TILES_DEV // 4, TILES_DEV + 1).astype(jnp.int32)
    chosen = jax.random.randint(jax.random.fold_in(key, 7), (), 0, grid).astype(jnp.int32)
    flat = jnp.arange(grid, dtype=jnp.int32)
    counts = jnp.where(flat == chosen, TILES_DEV, counts)
    counts = jnp.where(flat == (chosen + 1) % grid, TILES_DEV // 4, counts)
    return counts.reshape(ROW_GROUPS, COL_GROUPS).astype(jnp.int32)


def block_scale(rng, dims, cuts, low, high):
    gain, own = 1.0, jax.random.fold_in(rng, 6)
    for dim, blocks in cuts:
        draws = jnp.exp(jax.random.uniform(jax.random.fold_in(own, dim), (blocks,), jnp.float32, low / len(cuts), high / len(cuts)))
        gain = gain * jnp.repeat(draws, dims[dim] // blocks).reshape([-1 if axis == dim else 1 for axis in range(len(dims))])
    return gain


def normal_values(rng, shape, deviation, most, shards=(), kind=jnp.bfloat16):
    entries = jax.random.normal(rng, shape, jnp.float32) * deviation
    if len(shards) > 0:
        entries = block_scale(rng, shape, shards, -0.22, 0.18) * entries
    return jnp.clip(entries, min=-most, max=most).astype(kind)


def setup_inputs(seed: int = 0) -> dict:
    splits = jax.random.split(jax.random.key(seed), 8)
    features = normal_values(splits[0], (NODES, FEAT), 1.0, 6.0, ((0, 256),))
    weight = normal_values(splits[1], (FEAT, FEAT), FEAT ** -0.5, 0.375)
    cotangent = normal_values(splits[2], (NODES, FEAT), 1.0, 6.0, ((0, 256),))
    tile_rows = draw_tile_rows(jax.random.fold_in(splits[7], 71), 0)
    tile_cols = draw_tile_cols(jax.random.fold_in(splits[7], 71), 0)
    tile_values = normal_values(splits[5], (ROW_GROUPS, COL_GROUPS, TILES_DEV, TILE, TILE), (TILES_DEV * TILE // BLK_DEV) ** -0.5, 0.09375, ((0, 8), (1, 32)))
    tile_count = draw_tile_count(jax.random.fold_in(splits[7], 71), 0)
    return dict(features=features, weight=weight, cotangent=cotangent, tile_rows=tile_rows, tile_cols=tile_cols, tile_values=tile_values, tile_count=tile_count)


def positions(place, rows, cols):
    group_row = place // COL_GROUPS
    group_col = place % COL_GROUPS
    block_row = group_row * ROW_BLOCKS + rows
    block_col = ((cols // BLK_DEV) * COL_GROUPS + group_col) * BLK_DEV + cols % BLK_DEV
    return block_row.astype(jnp.int32), block_col.astype(jnp.int32)


def reference(features, weight, cotangent, tile_rows, tile_cols, tile_values, tile_count):
    blocks_all = NODES // TILE
    grid = ROW_GROUPS * COL_GROUPS
    flat_rows = tile_rows.reshape(grid, TILES_DEV)
    flat_cols = tile_cols.reshape(grid, TILES_DEV)
    flat_values = tile_values.reshape(grid, TILES_DEV, TILE, TILE)
    flat_counts = tile_count.reshape(grid)
    places = jnp.arange(grid, dtype=jnp.int32)
    slots = jnp.arange(TILES_DEV, dtype=jnp.int32)
    feat_blocks = features.reshape(blocks_all, TILE, FEAT)

    def forward_step(total, item):
        place, rows, cols, values, count = item
        block_row, block_col = positions(place, rows, cols)
        live = (slots < count).astype(jnp.float32)
        terms = jnp.einsum("tij,tjf->tif", values.astype(jnp.float32), feat_blocks[block_col].astype(jnp.float32), precision=lax.Precision.HIGHEST)
        return total.at[block_row].add(terms * live[:, None, None]), None

    zeros = jnp.zeros((blocks_all, TILE, FEAT), jnp.float32)
    items = (places, flat_rows, flat_cols, flat_values, flat_counts)
    summed, _ = lax.scan(forward_step, zeros, items)
    summed = summed.reshape(NODES, FEAT).astype(jnp.bfloat16)
    pre = jnp.dot(summed, weight, preferred_element_type=jnp.float32)
    sig = jax.nn.sigmoid(pre)
    hidden = (pre * sig).astype(jnp.bfloat16)
    grad_pre = (cotangent.astype(jnp.float32) * sig * (1.0 + pre * (1.0 - sig))).astype(jnp.bfloat16)
    grad_weight = jnp.dot(summed.T, grad_pre, preferred_element_type=jnp.float32)
    grad_summed = jnp.dot(grad_pre, weight.T, preferred_element_type=jnp.float32).astype(jnp.bfloat16)
    grad_blocks = grad_summed.reshape(blocks_all, TILE, FEAT)

    def backward_step(total, item):
        place, rows, cols, values, count = item
        block_row, block_col = positions(place, rows, cols)
        live = (slots < count).astype(jnp.float32)
        terms = jnp.einsum("tji,tjf->tif", values.astype(jnp.float32), grad_blocks[block_row].astype(jnp.float32), precision=lax.Precision.HIGHEST)
        return total.at[block_col].add(terms * live[:, None, None]), None

    grad_feat, _ = lax.scan(backward_step, zeros, items)
    grad_feat = grad_feat.reshape(NODES, FEAT).astype(jnp.bfloat16)
    return (hidden, grad_feat, grad_weight)
```

```python
import functools

import jax
import jax.numpy as jnp
from jax import lax
from jax.experimental import pallas as pl
from jax.experimental.pallas import tpu as pltpu
from jax.sharding import PartitionSpec as P

MESH = pl.DeviceIdType.MESH
BF16 = jnp.bfloat16
F32 = jnp.float32
T = 128
HALF = 128
COPIES = 340
GROUP = 8
URGENT = (4, 3, 5, 2, 6, 1, 7, 0)


def position():
    row, col = lax.axis_index("row"), lax.axis_index("col")
    return dict(
        x_hi=col // 16, z=lax.rem(col // 2, 8), core=lax.rem(col, 2), y=row // 2, x_lo=lax.rem(row, 2)
    )


def device(here, x_hi=0, x_lo=0, y=0, z=0, core=0):
    x_hi = 1 - here["x_hi"] if x_hi else here["x_hi"]
    x_lo = 1 - here["x_lo"] if x_lo else here["x_lo"]
    core = 1 - here["core"] if core else here["core"]
    y = lax.rem(here["y"] + y, 4)
    z = lax.rem(here["z"] + z, 8)
    return (y * 2 + x_lo, x_hi * 16 + z * 2 + core)


ROW_TILE, ROW_FEAT, ROW_KEEP, ROW_LAST, COL_TILE, COL_GRAD, COL_KEEP, COL_LAST = range(8)


def order_kernel(count_ref, rows_ref, cols_ref, table_ref):
    here = position()
    lane = lax.broadcasted_iota(jnp.int32, (T, T), 1)
    sub = lax.broadcasted_iota(jnp.int32, (T, T), 0)
    eye = lane == sub
    count = count_ref[0, 0]

    def spread(values):
        return jnp.broadcast_to(values, (T, T))

    def column(values):
        kept = jnp.where(eye, spread(values), 0).astype(F32)
        return jnp.broadcast_to(jnp.sum(kept, axis=1, keepdims=True), (T, T)).astype(jnp.int32)

    def total(values):
        return jnp.sum(values.astype(F32), axis=0, keepdims=True).astype(jnp.int32)

    live_down = sub < count

    def feat_place(cols):
        owner = cols // 4
        return ((lax.rem(owner, 2) + here["x_lo"]) % 2 * 4 + (owner // 2 - here["y"] + 4) % 4) * 4 + lax.rem(cols, 4)

    def grad_place(rows):
        owner, block = rows // 4, lax.rem(rows, 4)
        x_other = (owner // 16 + here["x_hi"]) % 2
        z_away = (lax.rem(owner // 2, 8) - here["z"] + 8) % 8
        core_other = (lax.rem(owner, 2) + here["core"]) % 2
        place = jnp.where(block < 2, 2 * block + x_other, 2 + block + 2 * x_other)
        return (core_other * 8 + z_away) * 8 + place

    rows, cols = rows_ref[...], cols_ref[...]
    rows_down, cols_down = grad_place(column(rows)), feat_place(column(cols))
    rows, cols = grad_place(rows), feat_place(cols)

    def sorted_by(keys, keys_down, value_down):
        big = T * T
        key = jnp.where(lane < count, spread(keys) * T + lane, big + lane)
        key_down = jnp.where(live_down, keys_down * T + sub, big + sub)
        rank_down = jnp.sum((key < key_down).astype(F32), axis=1, keepdims=True)
        rank_down = jnp.broadcast_to(rank_down, (T, T)).astype(jnp.int32)
        now = rank_down == lane
        tile = total(jnp.where(now, sub, 0))
        value = total(jnp.where(now, value_down, 0))
        mine = total(jnp.where(now, keys_down, 0))
        before = total(jnp.where(rank_down == lane - 1, keys_down, 0))
        first = lax.broadcasted_iota(jnp.int32, (1, T), 1) == 0
        keep = jnp.where(jnp.logical_or(first, mine != before), 0, 1)
        upto = total(jnp.where(jnp.logical_and(live_down, keys_down <= lane), 1, 0))
        some = total(jnp.where(jnp.logical_and(live_down, keys_down == lane), 1, 0))
        return [tile, value, keep, jnp.where(some > 0, upto - 1, T)]

    lines = sorted_by(rows, rows_down, cols_down) + sorted_by(cols, cols_down, rows_down)
    for number, line in enumerate(lines):
        table_ref[number : number + 1, :] = line


def each(count, body):
    def step(i, carried):
        body(i)
        return carried

    lax.fori_loop(0, count, step, 0)


def add_up(out, terms):
    def body(i):
        rows = pl.ds(i * 32, 32)
        total = terms[0][:, rows].astype(F32)
        for term in terms[1:]:
            total = total + term[:, rows].astype(F32)
        out[:, rows] = total.astype(out.dtype)

    each(T // 32, body)


class Links:
    def __init__(self, send_sem, recv_sem):
        self.send_sem, self.recv_sem, self.copies = send_sem, recv_sem, []

    def send(self, src, dst, to):
        number = len(self.copies)
        copy = pltpu.make_async_remote_copy(
            src_ref=src,
            dst_ref=dst,
            send_sem=self.send_sem.at[number],
            recv_sem=self.recv_sem.at[number],
            device_id=to,
            device_id_type=MESH,
        )
        copy.start()
        self.copies.append(copy)
        return copy


def layer_kernel(
    table,
    feat_hbm,
    weight,
    cot_hbm,
    tile_hbm,
    hidden,
    grad_feat,
    grad_weight,
    tiles,
    cot,
    feats0,
    feats1,
    slots,
    give,
    core_in,
    value,
    x_in,
    ring_in,
    x_last,
    part,
    summed,
    grads0,
    grads1,
    carry,
    back,
    back_x,
    back_y,
    back_y2,
    back_x2,
    w_sum,
    w_own,
    w_core,
    w_y,
    w_z,
    w_x,
    w_all_z,
    w_all_y,
    w_all,
    local_sem,
    send_sem,
    recv_sem,
):
    here = position()
    feats, grads = (feats0, feats1), (grads0, grads1)
    links = Links(send_sem, recv_sem)
    z_up, z_down = device(here, z=1), device(here, z=7)
    x_far, x_near = device(here, x_hi=1), device(here, x_lo=1)
    x_both = device(here, x_hi=1, x_lo=1)
    twin = device(here, core=1)
    y_to = {d: device(here, y=d) for d in (1, 2, 3)}
    z_to = {d: device(here, z=d) for d in range(1, 8)}

    loads = [
        pltpu.make_async_copy(feat_hbm.at[:, :, pl.ds(f * HALF, HALF)], feats[f].at[pl.ds(0, 4)], local_sem.at[f])
        for f in range(2)
    ]
    loads.append(pltpu.make_async_copy(tile_hbm, tiles, local_sem.at[2]))
    loads.append(pltpu.make_async_copy(cot_hbm, cot, local_sem.at[3]))
    for load in loads:
        load.start()

    barrier = pltpu.get_barrier_semaphore()
    partners = [x_far, x_near, x_both, twin, *y_to.values(), *z_to.values()]
    for partner in partners:
        pl.semaphore_signal(barrier, inc=1, device_id=partner, device_id_type=MESH)
    for f in range(2):
        slots[f, T] = jnp.zeros((T, HALF), BF16)
    loads[0].wait()
    loads[1].wait()
    pl.semaphore_wait(barrier, len(partners))

    def gather_first(f):
        own = feats[f].at[pl.ds(0, 4)]
        near = links.send(own, feats[f].at[pl.ds(16, 4)], x_near)
        over = {d: links.send(own, feats[f].at[pl.ds((4 - d) * 4, 4)], y_to[d]) for d in (1, 3, 2)}
        return near, over

    def gather_second(f, first):
        near, over = first
        near.wait_recv()
        copies = [
            links.send(feats[f].at[pl.ds(16, 2)], feats[f].at[pl.ds(16 + (4 - d) * 4, 2)], y_to[d])
            for d in (1, 3, 2)
        ]
        for d in (1, 3, 2):
            over[d].wait_recv()
            rows = (4 - d) * 4 + 2
            copies.append(links.send(feats[f].at[pl.ds(rows, 2)], feats[f].at[pl.ds(16 + rows, 2)], x_near))
        return copies

    def products(f, piece, pieces, back_pass):
        tile_line, value_line, keep_line = (
            (COL_TILE, COL_GRAD, COL_KEEP) if back_pass else (ROW_TILE, ROW_FEAT, ROW_KEEP)
        )
        steps = T // GROUP // pieces
        source = (grads if back_pass else feats)[f]

        def step(i):
            total = carry[...]
            for u in range(GROUP):
                t = i * GROUP + u
                tile = tiles[table[tile_line, t]]
                block = source[table[value_line, t]]
                if back_pass:
                    tile = tile.T
                term = jnp.dot(tile, block, preferred_element_type=F32)
                total = term + total * table[keep_line, t].astype(F32)
                slots[f, t] = total.astype(BF16)
            carry[...] = total

        each(steps, lambda i: step(piece * steps + i))

    def core_send(f):
        copies = {}
        for dz in URGENT:

            def fill(place, dz=dz):
                give[f, dz * 8 + place] = slots[f, table[ROW_LAST, 64 + dz * 8 + place]]

            each(8, fill)
            span = pl.ds(dz * 8, 8)
            copies[dz] = links.send(give.at[f, span], core_in.at[f, span], twin)
        return copies

    def core_sum(f, dz, copies):
        copies[dz].wait_recv()

        def fill(place):
            at = dz * 8 + place
            own = slots[f, table[ROW_LAST, at]].astype(F32)
            value[f, at] = (own + core_in[f, at].astype(F32)).astype(BF16)

        each(8, fill)
        return links.send(value.at[f, pl.ds(dz * 8 + 6, 2)], x_in.at[f, pl.ds(dz * 2, 2)], x_far)

    class Ring:
        def __init__(self, f, stream, x_copies=None):
            self.f, self.stream, self.x_copies = f, stream, x_copies
            self.up = self.down = None

        def span(self, dz, first=0, size=2):
            return value.at[self.f, pl.ds(dz * 8 + self.stream * 2 + first, size)]

        def own(self, dz, first=0, size=2):
            if self.x_copies is None:
                return [self.span(dz, first, size)]
            return [self.span(dz, first, size), x_in.at[self.f, pl.ds(dz * 2 + first, size)]]

        def slot(self, way, step, first=0, size=2):
            return ring_in.at[self.f, self.stream, way, pl.ds(step * 2 + first, size)]

        def step(self, s):
            if s == 0:
                if self.x_copies is not None:
                    self.x_copies[4].wait_recv()
                    add_up(self.span(4), self.own(4))
                self.up = links.send(self.span(4, 0, 1), self.slot(0, 0, 0, 1), z_up)
                self.down = links.send(self.span(4, 1, 1), self.slot(1, 0, 1, 1), z_down)
                return
            for way, dz in ((0, 4 - s), (1, 4 + s)):
                if self.x_copies is not None:
                    self.x_copies[dz].wait_recv()
                (self.up, self.down)[way].wait_recv()
                if s == 1:
                    add_up(self.span(dz, way, 1), self.own(dz, way, 1) + [self.slot(way, 0, way, 1)])
                    if self.x_copies is not None:
                        add_up(self.span(dz, 1 - way, 1), self.own(dz, 1 - way, 1))
                else:
                    add_up(self.span(dz), self.own(dz) + [self.slot(way, s - 1)])
                sent = links.send(self.span(dz), self.slot(way, s), (z_up, z_down)[way])
                if way == 0:
                    self.up = sent
                else:
                    self.down = sent

        def finish(self):
            if self.x_copies is not None:
                self.x_copies[0].wait_recv()
            self.up.wait_recv()
            self.down.wait_recv()

        def last(self, first, size):
            return self.own(0, first, size) + [self.slot(0, 3, first, size), self.slot(1, 3, first, size)]

    def finish_z(f, b, ring):
        ring.finish()
        far = pl.ds(2 * f + b, 1)
        add_up(x_last.at[0, far], ring.last(1, 1))
        copy = links.send(x_last.at[0, far], x_last.at[1, far], x_far)
        add_up(part.at[f, pl.ds(b, 1)], ring.last(0, 1))
        return copy

    def close_z(f, b, copy):
        copy.wait_recv()
        add_up(
            summed.at[pl.ds(b, 1), :, pl.ds(f * HALF, HALF)],
            [part.at[f, pl.ds(b, 1)], x_last.at[1, pl.ds(2 * f + b, 1)]],
        )

    def close_x(f, ring):
        ring.finish()
        add_up(summed.at[pl.ds(2, 2), :, pl.ds(f * HALF, HALF)], ring.last(0, 2))

    def middle(pair):
        def body(i):
            b = 2 * pair + i
            rows = summed[b]
            pre = jnp.dot(rows, weight[...], preferred_element_type=F32)
            sig = jax.nn.sigmoid(pre)
            hidden[b] = (pre * sig).astype(BF16)
            grad_pre = (cot[b].astype(F32) * sig * (1.0 + pre * (1.0 - sig))).astype(BF16)
            own = lax.dot_general(
                grad_pre, weight[...], (((1,), (1,)), ((), ())), preferred_element_type=F32
            )
            place = 2 * i if pair == 0 else 4 + i
            for f in range(2):
                grads[f][place] = own[:, f * HALF : (f + 1) * HALF].astype(BF16)
            w_sum[...] += jnp.dot(rows.T, grad_pre, preferred_element_type=F32)

        each(2, body)

    first = gather_first(0)
    second = gather_second(0, first)
    first1 = gather_first(1)
    loads[2].wait()
    loads[3].wait()
    w_sum[...] = jnp.zeros_like(w_sum)
    carry[...] = jnp.zeros_like(carry)
    for copy in second:
        copy.wait_recv()
    products(0, 0, 1, False)
    core0 = core_send(0)
    second1 = gather_second(1, first1)
    x0 = {}
    z0 = [Ring(0, 0), Ring(0, 1)]
    for dz in URGENT:
        x0[dz] = core_sum(0, dz, core0)
        if dz == 4:
            for ring in z0:
                ring.step(0)
    for ring in z0:
        ring.step(1)
    for copy in second1:
        copy.wait_recv()
    for piece in range(2):
        products(1, piece, 2, False)
        for ring in z0:
            ring.step(2 + piece)
    core1 = core_send(1)
    last = {}
    for b in range(2):
        last[0, b] = finish_z(0, b, z0[b])
    x1 = {}
    ring_x0 = Ring(0, 2, x0)
    z1 = [Ring(1, 0), Ring(1, 1)]
    ring_x0.step(0)
    for dz in URGENT:
        x1[dz] = core_sum(1, dz, core1)
        if dz == 4:
            for ring in z1:
                ring.step(0)
    for s in range(1, 4):
        ring_x0.step(s)
        for ring in z1:
            ring.step(s)
    ring_x1 = Ring(1, 2, x1)
    ring_x1.step(0)
    close_x(0, ring_x0)
    for b in range(2):
        last[1, b] = finish_z(1, b, z1[b])
    ring_x1.step(1)
    for b in range(2):
        for f in range(2):
            close_z(f, b, last[f, b])
    ring_x1.step(2)
    ring_x1.step(3)
    middle(0)

    def spread_near(f, b):
        return links.send(grads[f].at[pl.ds(2 * b, 1)], grads[f].at[pl.ds(2 * b + 1, 1)], x_far)

    class Spread:
        def __init__(self, f, stream):
            self.f, self.stream = f, stream
            self.up = self.down = None

        def span(self, dz, first=0, size=2):
            return self.at(self.f, dz, self.stream * 2 + first, size)

        @staticmethod
        def at(f, dz, place, size):
            return grads[f].at[pl.ds((dz % 8) * 8 + place, size)]

        def step(self, s):
            if s > 0:
                self.up.wait_recv()
                self.down.wait_recv()
            first, size = ((0, 2), (1, 1))[s == 3]
            self.up = links.send(
                self.span(-s, 0, size), self.span(-s - 1, 0, size), z_up
            )
            self.down = links.send(self.span(s, first, size), self.span(s + 1, first, size), z_down)

        def done(self):
            self.up.wait_recv()
            self.down.wait_recv()

    def to_twin(f, dz, place, size):
        at = (dz % 8) * 8 + place
        return links.send(grads[f].at[pl.ds(at, size)], grads[f].at[pl.ds(64 + at, size)], twin)

    def to_far(f, dz):
        at = (dz % 8) * 8
        return links.send(grads[f].at[pl.ds(at + 4, 2)], grads[f].at[pl.ds(at + 6, 2)], x_far)

    near = {(f, b): spread_near(f, b) for f in range(2) for b in range(2)}
    close_x(1, ring_x1)
    middle(1)
    streams = {f: [Spread(f, 0), Spread(f, 1), Spread(f, 2)] for f in range(2)}
    from_far = {0: {}, 1: {}}
    from_twin = {0: [], 1: []}

    def round_of(f, s):
        for k in (2, 0, 1):
            if s == 0 and k < 2:
                near[f, k].wait_recv()
            if s < 4:
                streams[f][k].step(s)
            else:
                streams[f][k].done()
            if k == 2:
                for dz in sorted({-s % 8, s % 8}):
                    from_far[f][dz] = to_far(f, dz)
                    from_twin[f].append(to_twin(f, dz, 4, 2))
        for dz in sorted({-s % 8, s % 8}):
            from_twin[f].append(to_twin(f, dz, 0, 4))

    def far_to_twin(f, dzs):
        for dz in dzs:
            from_far[f][dz % 8].wait_recv()
            from_twin[f].append(to_twin(f, dz, 6, 2))

    def all_here(f):
        for copy in from_twin[f]:
            copy.wait_recv()

    def weight_start():
        def fill(i):
            for j in range(2):
                w_own[2 * i + j] = w_sum[pl.ds(8 * i, 8), j * 128 : (j + 1) * 128]

        each(32, fill)
        return links.send(w_own.at[pl.ds((1 - here["core"]) * 32, 32)], w_core.at[0], twin)

    def weight_y(copy):
        copy.wait_recv()

        def fill(i):
            w_core[1, i] = w_own[here["core"] * 32 + i] + w_core[0, i]

        each(32, fill)
        return [
            links.send(w_core.at[1, pl.ds(lax.rem(here["y"] + d, 4) * 8, 8)], w_y.at[d], y_to[d]) for d in (1, 2, 3)
        ]

    def weight_z(copies):
        for copy in copies:
            copy.wait_recv()

        def fill(i):
            w_y[0, i] = w_core[1, here["y"] * 8 + i] + w_y[1, i] + w_y[2, i] + w_y[3, i]

        each(8, fill)
        return [
            links.send(w_y.at[0, pl.ds(lax.rem(here["z"] + d, 8), 1)], w_z.at[pl.ds(d, 1)], z_to[d])
            for d in range(1, 8)
        ]

    def weight_x(copies):
        for copy in copies:
            copy.wait_recv()
        total = w_y[0, pl.ds(here["z"], 1)]
        for d in range(1, 8):
            total = total + w_z[d : d + 1]
        w_x[0:1] = total
        return [
            links.send(w_x.at[pl.ds(0, 1)], w_x.at[pl.ds(i, 1)], to)
            for i, to in ((1, x_far), (2, x_near), (3, x_both))
        ]

    def weight_all_z(copies):
        for copy in copies:
            copy.wait_recv()
        mine = pl.ds(here["z"], 1)
        w_all_z[mine] = (w_x[0:1] + w_x[1:2]) + (w_x[2:3] + w_x[3:4])
        return [links.send(w_all_z.at[mine], w_all_z.at[mine], z_to[d]) for d in range(1, 8)]

    def weight_all_y(copies):
        for copy in copies:
            copy.wait_recv()
        mine = pl.ds(here["y"] * 8, 8)

        def fill(i):
            w_all_y[here["y"] * 8 + i] = w_all_z[i]

        each(8, fill)
        return [links.send(w_all_y.at[mine], w_all_y.at[mine], y_to[d]) for d in (1, 2, 3)]

    def weight_all_core(copies):
        for copy in copies:
            copy.wait_recv()
        mine = pl.ds(here["core"] * 32, 32)

        def fill(i):
            w_all[here["core"] * 32 + i] = w_all_y[i]

        each(32, fill)
        return links.send(w_all.at[mine], w_all.at[mine], twin)

    def weight_end(copy):
        copy.wait_recv()

        def fill(i):
            for j in range(2):
                grad_weight[pl.ds(8 * i, 8), j * 128 : (j + 1) * 128] = w_all[2 * i + j]

        each(32, fill)

    def back_first(f):
        def fill(place):
            back[f, place] = slots[f, table[COL_LAST, place]]

        each(32, fill)
        near_copies = {
            d: links.send(back.at[f, pl.ds((4 + d) * 4, 2)], back_x.at[f, pl.ds(d * 2, 2)], x_near)
            for d in (2, 1, 3, 0)
        }
        y_copies = [
            links.send(back.at[f, pl.ds((x_other * 4 + d) * 4 + 2, 2)], back_y.at[f, d, pl.ds(x_other * 2, 2)], y_to[d])
            for x_other in (1, 0)
            for d in (2, 1, 3)
        ]
        return near_copies, y_copies

    def back_second(f, first):
        near_copies, y_copies = first
        y_second = []
        for d in (2, 1, 3, 0):
            near_copies[d].wait_recv()
            own = back.at[f, pl.ds(d * 4, 2)]
            add_up(own, [own, back_x.at[f, pl.ds(d * 2, 2)]])
            if d:
                y_second.append(links.send(back.at[f, pl.ds(d * 4, 2)], back_y2.at[f, d], y_to[d]))
        for copy in y_copies[:3]:
            copy.wait_recv()
        add_up(
            back_x2.at[f, pl.ds(0, 2)],
            [back.at[f, pl.ds(18, 2)]] + [back_y.at[f, d, pl.ds(2, 2)] for d in (1, 2, 3)],
        )
        near_second = links.send(back_x2.at[f, pl.ds(0, 2)], back_x2.at[f, pl.ds(2, 2)], x_near)
        return y_copies[3:], y_second, near_second

    def back_third(f, second):
        y_copies, y_second, near_second = second
        lanes = pl.ds(f * HALF, HALF)
        for copy in y_copies + [near_second]:
            copy.wait_recv()
        add_up(
            grad_feat.at[pl.ds(2, 2), :, lanes],
            [back.at[f, pl.ds(2, 2)], back_x2.at[f, pl.ds(2, 2)]]
            + [back_y.at[f, d, pl.ds(0, 2)] for d in (1, 2, 3)],
        )
        for copy in y_second:
            copy.wait_recv()
        add_up(
            grad_feat.at[pl.ds(0, 2), :, lanes],
            [back.at[f, pl.ds(0, 2)]] + [back_y2.at[f, d] for d in (1, 2, 3)],
        )

    round_of(0, 0)
    w_copy = weight_start()
    round_of(0, 1)
    w_copy = weight_y(w_copy)
    round_of(0, 2)
    far_to_twin(0, (0,))
    round_of(0, 3)
    w_copy = weight_z(w_copy)
    round_of(1, 0)
    far_to_twin(0, (1, 7))
    round_of(0, 4)
    round_of(1, 1)
    w_copy = weight_x(w_copy)
    far_to_twin(0, (2, 6))
    round_of(1, 2)
    far_to_twin(0, (3, 5, 4))
    w_copy = weight_all_z(w_copy)
    all_here(0)
    products(0, 0, 2, True)
    round_of(1, 3)
    products(0, 1, 2, True)
    w_copy = weight_all_y(w_copy)
    first0 = back_first(0)
    round_of(1, 4)
    far_to_twin(1, (0, 1, 7, 2, 6))
    second0 = back_second(0, first0)
    w_copy = weight_all_core(w_copy)
    far_to_twin(1, (3, 5, 4))
    all_here(1)
    products(1, 0, 1, True)
    first1 = back_first(1)
    weight_end(w_copy)
    back_third(0, second0)
    back_third(1, back_second(1, first1))
    for copy in links.copies:
        copy.wait_send()


def per_device(features, weight, cotangent, tile_rows, tile_cols, tile_values, tile_count):
    table = pl.pallas_call(
        order_kernel,
        out_shape=jax.ShapeDtypeStruct((8, T), jnp.int32),
        in_specs=[
            pl.BlockSpec(memory_space=pltpu.SMEM),
            pl.BlockSpec(memory_space=pltpu.VMEM),
            pl.BlockSpec(memory_space=pltpu.VMEM),
        ],
        out_specs=pl.BlockSpec(memory_space=pltpu.VMEM),
        name="order",
    )(tile_count, tile_rows.reshape(1, T), tile_cols.reshape(1, T))
    hbm, vmem = pl.BlockSpec(memory_space=pl.ANY), pl.BlockSpec(memory_space=pltpu.VMEM)

    def blocks(*counts):
        return pltpu.VMEM((*counts, T, HALF), BF16)

    def pieces(*counts):
        return pltpu.VMEM((*counts, 8, 128), F32)

    hidden, grad_feat, grad_weight = pl.pallas_call(
        layer_kernel,
        out_shape=(
            jax.ShapeDtypeStruct((4, T, 256), BF16),
            jax.ShapeDtypeStruct((4, T, 256), BF16),
            jax.ShapeDtypeStruct((256, 256), F32),
        ),
        in_specs=[pl.BlockSpec(memory_space=pltpu.SMEM), hbm, vmem, hbm, hbm],
        out_specs=(vmem, vmem, vmem),
        scratch_shapes=[
            blocks(T),
            pltpu.VMEM((4, T, 256), BF16),
            blocks(32),
            blocks(32),
            blocks(2, T + 1),
            blocks(2, 64),
            blocks(2, 64),
            blocks(2, 64),
            blocks(2, 16),
            blocks(2, 3, 2, 8),
            blocks(2, 4),
            pltpu.VMEM((2, 2, T, HALF), F32),
            pltpu.VMEM((4, T, 256), BF16),
            blocks(128),
            blocks(128),
            pltpu.VMEM((T, HALF), F32),
            blocks(2, 32),
            blocks(2, 8),
            blocks(2, 4, 4),
            blocks(2, 4, 2),
            blocks(2, 4),
            pltpu.VMEM((256, 256), F32),
            pieces(64),
            pieces(2, 32),
            pieces(4, 8),
            pieces(8),
            pieces(4),
            pieces(8),
            pieces(32),
            pieces(64),
            pltpu.SemaphoreType.DMA((4,)),
            pltpu.SemaphoreType.DMA((COPIES,)),
            pltpu.SemaphoreType.DMA((COPIES,)),
        ],
        compiler_params=pltpu.CompilerParams(
            collective_id=0, has_side_effects=True, vmem_limit_bytes=60 * 2**20
        ),
        cost_estimate=pl.CostEstimate(flops=5 * 10**9, bytes_accessed=6 * 2**20, transcendentals=2**17),
        name="layer",
    )(
        table,
        features.reshape(4, T, 256),
        weight,
        cotangent.reshape(4, T, 256),
        tile_values.reshape(T, T, T),
    )
    return hidden.reshape(4 * T, 256), grad_feat.reshape(4 * T, 256), grad_weight


def solution(mesh):
    placed = (
        P(("row", "col"), None),
        P(),
        P(("row", "col"), None),
        P("row", "col", None),
        P("row", "col", None),
        P("row", "col", None, None, None),
        P("row", "col"),
    )
    return jax.shard_map(
        per_device,
        mesh=mesh,
        in_specs=placed,
        out_specs=(P(("row", "col"), None), P(("row", "col"), None), P()),
        check_vma=False,
    )
```

```python
import functools

import jax
import jax.numpy as jnp
from jax import lax
from jax.experimental import pallas as pl
from jax.experimental.pallas import tpu as pltpu
from jax.sharding import PartitionSpec as P

MESH = pl.DeviceIdType.MESH
BF16 = jnp.bfloat16
F32 = jnp.float32
T = 128
HALF = 128
COPIES = 340
GROUP = 8
URGENT = (4, 3, 5, 2, 6, 1, 7, 0)


def position():
    row, col = lax.axis_index("row"), lax.axis_index("col")
    return dict(
        x_hi=col // 16, z=lax.rem(col // 2, 8), core=lax.rem(col, 2), y=row // 2, x_lo=lax.rem(row, 2)
    )


def device(here, x_hi=0, x_lo=0, y=0, z=0, core=0):
    x_hi = 1 - here["x_hi"] if x_hi else here["x_hi"]
    x_lo = 1 - here["x_lo"] if x_lo else here["x_lo"]
    core = 1 - here["core"] if core else here["core"]
    y = lax.rem(here["y"] + y, 4)
    z = lax.rem(here["z"] + z, 8)
    return (y * 2 + x_lo, x_hi * 16 + z * 2 + core)


ROW_TILE, ROW_KEEP, ROW_LAST, ROW_FEAT, COL_TILE, COL_KEEP, COL_LAST, COL_GRAD = range(8)
LINES = 9


def order_kernel(count_ref, rows_ref, cols_ref, table_ref):
    here = position()
    lane = lax.broadcasted_iota(jnp.int32, (T, T), 1)
    sub = lax.broadcasted_iota(jnp.int32, (T, T), 0)
    eye = lane == sub
    count = count_ref[0, 0]

    def spread(values):
        return jnp.broadcast_to(values, (T, T))

    def column(values):
        kept = jnp.where(eye, spread(values), 0).astype(F32)
        return jnp.broadcast_to(jnp.sum(kept, axis=1, keepdims=True), (T, T)).astype(jnp.int32)

    def total(values):
        return jnp.sum(values.astype(F32), axis=0, keepdims=True).astype(jnp.int32)

    live_down = sub < count

    def feat_place(cols):
        owner = cols // 4
        return ((lax.rem(owner, 2) + here["x_lo"]) % 2 * 4 + (owner // 2 - here["y"] + 4) % 4) * 4 + lax.rem(cols, 4)

    def row_place(rows, order):
        owner, block = rows // 4, lax.rem(rows, 4)
        x_other = (owner // 16 + here["x_hi"]) % 2
        z_away = (lax.rem(owner // 2, 8) - here["z"] + 8) % 8
        core_other = (lax.rem(owner, 2) + here["core"]) % 2
        return (core_other * 8 + z_away) * 8 + order(block, x_other)

    def sum_order(block, x_other):
        return jnp.where(block < 2, 2 * block + x_other, 2 + block + 2 * x_other)

    def far_last(block, x_other):
        return block + 4 * x_other

    def far_first(block, x_other):
        return 2 * block + x_other

    rows, cols = rows_ref[...], cols_ref[...]
    rows_down, cols_down = column(rows), feat_place(column(cols))
    grads_down = [row_place(rows_down, far_last), row_place(rows_down, far_first)]
    rows_down = row_place(rows_down, sum_order)
    rows, cols = row_place(rows, sum_order), feat_place(cols)

    def sorted_by(keys, keys_down, values_down):
        big = T * T
        key = jnp.where(lane < count, spread(keys) * T + lane, big + lane)
        key_down = jnp.where(live_down, keys_down * T + sub, big + sub)
        rank_down = jnp.sum((key < key_down).astype(F32), axis=1, keepdims=True)
        rank_down = jnp.broadcast_to(rank_down, (T, T)).astype(jnp.int32)
        now = rank_down == lane
        tile = total(jnp.where(now, sub, 0))
        values = [total(jnp.where(now, value, 0)) for value in values_down]
        mine = total(jnp.where(now, keys_down, 0))
        before = total(jnp.where(rank_down == lane - 1, keys_down, 0))
        first = lax.broadcasted_iota(jnp.int32, (1, T), 1) == 0
        keep = jnp.where(jnp.logical_or(first, mine != before), 0, 1)
        upto = total(jnp.where(jnp.logical_and(live_down, keys_down <= lane), 1, 0))
        some = total(jnp.where(jnp.logical_and(live_down, keys_down == lane), 1, 0))
        return [tile, keep, jnp.where(some > 0, upto - 1, T), *values]

    lines = sorted_by(rows, rows_down, [cols_down]) + sorted_by(cols, cols_down, grads_down)
    for number, line in enumerate(lines):
        table_ref[number : number + 1, :] = line


def each(count, body):
    def step(i, carried):
        body(i)
        return carried

    lax.fori_loop(0, count, step, 0)


def add_up(out, terms):
    def body(i):
        rows = pl.ds(i * 32, 32)
        total = terms[0][:, rows].astype(F32)
        for term in terms[1:]:
            total = total + term[:, rows].astype(F32)
        out[:, rows] = total.astype(out.dtype)

    each(T // 32, body)


class Links:
    def __init__(self, send_sem, recv_sem):
        self.send_sem, self.recv_sem, self.copies = send_sem, recv_sem, []

    def send(self, src, dst, to):
        number = len(self.copies)
        copy = pltpu.make_async_remote_copy(
            src_ref=src,
            dst_ref=dst,
            send_sem=self.send_sem.at[number],
            recv_sem=self.recv_sem.at[number],
            device_id=to,
            device_id_type=MESH,
        )
        copy.start()
        self.copies.append(copy)
        return copy


def layer_kernel(
    table,
    feat_hbm,
    weight,
    cot_hbm,
    tile_hbm,
    hidden,
    grad_feat,
    grad_weight,
    tiles,
    cot,
    feats0,
    feats1,
    slots,
    give,
    core_in,
    value,
    x_in,
    ring_in,
    x_last,
    part,
    summed,
    grads0,
    grads1,
    carry,
    back,
    back_x,
    back_y,
    back_y2,
    back_x2,
    w_sum,
    w_own,
    w_core,
    w_y,
    w_z,
    w_x,
    w_all_z,
    w_all_y,
    w_all,
    local_sem,
    send_sem,
    recv_sem,
):
    here = position()
    feats, grads = (feats0, feats1), (grads0, grads1)
    links = Links(send_sem, recv_sem)
    z_up, z_down = device(here, z=1), device(here, z=7)
    x_far, x_near = device(here, x_hi=1), device(here, x_lo=1)
    x_both = device(here, x_hi=1, x_lo=1)
    twin = device(here, core=1)
    y_to = {d: device(here, y=d) for d in (1, 2, 3)}
    z_to = {d: device(here, z=d) for d in range(1, 8)}

    loads = [
        pltpu.make_async_copy(feat_hbm.at[:, :, pl.ds(f * HALF, HALF)], feats[f].at[pl.ds(0, 4)], local_sem.at[f])
        for f in range(2)
    ]
    loads.append(pltpu.make_async_copy(tile_hbm, tiles, local_sem.at[2]))
    loads.append(pltpu.make_async_copy(cot_hbm, cot, local_sem.at[3]))
    for load in loads:
        load.start()

    barrier = pltpu.get_barrier_semaphore()
    partners = [x_far, x_near, x_both, twin, *y_to.values(), *z_to.values()]
    for partner in partners:
        pl.semaphore_signal(barrier, inc=1, device_id=partner, device_id_type=MESH)
    for f in range(2):
        slots[f, T] = jnp.zeros((T, HALF), BF16)
    loads[0].wait()
    loads[1].wait()
    pl.semaphore_wait(barrier, len(partners))

    def gather_first(f):
        own = feats[f].at[pl.ds(0, 4)]
        near = links.send(own, feats[f].at[pl.ds(16, 4)], x_near)
        over = {d: links.send(own, feats[f].at[pl.ds((4 - d) * 4, 4)], y_to[d]) for d in (1, 3, 2)}
        return near, over

    def gather_second(f, first):
        near, over = first
        near.wait_recv()
        copies = [
            links.send(feats[f].at[pl.ds(16, 2)], feats[f].at[pl.ds(16 + (4 - d) * 4, 2)], y_to[d])
            for d in (1, 3, 2)
        ]
        for d in (1, 3, 2):
            over[d].wait_recv()
            rows = (4 - d) * 4 + 2
            copies.append(links.send(feats[f].at[pl.ds(rows, 2)], feats[f].at[pl.ds(16 + rows, 2)], x_near))
        return copies

    def products(f, piece, pieces, back_pass):
        tile_line, value_line, keep_line = (
            (COL_TILE, COL_GRAD + f, COL_KEEP) if back_pass else (ROW_TILE, ROW_FEAT, ROW_KEEP)
        )
        steps = T // GROUP // pieces
        source = (grads if back_pass else feats)[f]

        def step(i):
            total = carry[...]
            for u in range(GROUP):
                t = i * GROUP + u
                tile = tiles[table[tile_line, t]]
                block = source[table[value_line, t]]
                if back_pass:
                    tile = tile.T
                term = jnp.dot(tile, block, preferred_element_type=F32)
                total = term + total * table[keep_line, t].astype(F32)
                slots[f, t] = total.astype(BF16)
            carry[...] = total

        each(steps, lambda i: step(piece * steps + i))

    def core_send(f):
        copies = {}
        for dz in URGENT:

            def fill(place, dz=dz):
                give[f, dz * 8 + place] = slots[f, table[ROW_LAST, 64 + dz * 8 + place]]

            each(8, fill)
            span = pl.ds(dz * 8, 8)
            copies[dz] = links.send(give.at[f, span], core_in.at[f, span], twin)
        return copies

    def core_sum(f, dz, copies):
        copies[dz].wait_recv()

        def fill(place):
            at = dz * 8 + place
            own = slots[f, table[ROW_LAST, at]].astype(F32)
            value[f, at] = (own + core_in[f, at].astype(F32)).astype(BF16)

        each(8, fill)
        return links.send(value.at[f, pl.ds(dz * 8 + 6, 2)], x_in.at[f, pl.ds(dz * 2, 2)], x_far)

    class Ring:
        def __init__(self, f, stream, x_copies=None):
            self.f, self.stream, self.x_copies = f, stream, x_copies
            self.up = self.down = None

        def span(self, dz, first=0, size=2):
            return value.at[self.f, pl.ds(dz * 8 + self.stream * 2 + first, size)]

        def own(self, dz, first=0, size=2):
            if self.x_copies is None:
                return [self.span(dz, first, size)]
            return [self.span(dz, first, size), x_in.at[self.f, pl.ds(dz * 2 + first, size)]]

        def slot(self, way, step, first=0, size=2):
            return ring_in.at[self.f, self.stream, way, pl.ds(step * 2 + first, size)]

        def step(self, s):
            if s == 0:
                if self.x_copies is not None:
                    self.x_copies[4].wait_recv()
                    add_up(self.span(4), self.own(4))
                self.up = links.send(self.span(4, 0, 1), self.slot(0, 0, 0, 1), z_up)
                self.down = links.send(self.span(4, 1, 1), self.slot(1, 0, 1, 1), z_down)
                return
            for way, dz in ((0, 4 - s), (1, 4 + s)):
                if self.x_copies is not None:
                    self.x_copies[dz].wait_recv()
                (self.up, self.down)[way].wait_recv()
                if s == 1:
                    add_up(self.span(dz, way, 1), self.own(dz, way, 1) + [self.slot(way, 0, way, 1)])
                    if self.x_copies is not None:
                        add_up(self.span(dz, 1 - way, 1), self.own(dz, 1 - way, 1))
                else:
                    add_up(self.span(dz), self.own(dz) + [self.slot(way, s - 1)])
                sent = links.send(self.span(dz), self.slot(way, s), (z_up, z_down)[way])
                if way == 0:
                    self.up = sent
                else:
                    self.down = sent

        def finish(self):
            if self.x_copies is not None:
                self.x_copies[0].wait_recv()
            self.up.wait_recv()
            self.down.wait_recv()

        def last(self, first, size):
            return self.own(0, first, size) + [self.slot(0, 3, first, size), self.slot(1, 3, first, size)]

    def finish_z(f, b, ring):
        ring.finish()
        far = pl.ds(2 * f + b, 1)
        add_up(x_last.at[0, far], ring.last(1, 1))
        copy = links.send(x_last.at[0, far], x_last.at[1, far], x_far)
        add_up(part.at[f, pl.ds(b, 1)], ring.last(0, 1))
        return copy

    def close_z(f, b, copy):
        copy.wait_recv()
        add_up(
            summed.at[pl.ds(b, 1), :, pl.ds(f * HALF, HALF)],
            [part.at[f, pl.ds(b, 1)], x_last.at[1, pl.ds(2 * f + b, 1)]],
        )

    def close_x(f, ring):
        ring.finish()
        add_up(summed.at[pl.ds(2, 2), :, pl.ds(f * HALF, HALF)], ring.last(0, 2))

    def middle(pair):
        def body(i):
            b = 2 * pair + i
            rows = summed[b]
            pre = jnp.dot(rows, weight[...], preferred_element_type=F32)
            sig = jax.nn.sigmoid(pre)
            hidden[b] = (pre * sig).astype(BF16)
            grad_pre = (cot[b].astype(F32) * sig * (1.0 + pre * (1.0 - sig))).astype(BF16)
            own = lax.dot_general(
                grad_pre, weight[...], (((1,), (1,)), ((), ())), preferred_element_type=F32
            )
            grads[0][b] = own[:, :HALF].astype(BF16)
            grads[1][2 * b] = own[:, HALF:].astype(BF16)
            w_sum[...] += jnp.dot(rows.T, grad_pre, preferred_element_type=F32)

        each(2, body)

    first = gather_first(0)
    second = gather_second(0, first)
    first1 = gather_first(1)
    loads[2].wait()
    loads[3].wait()
    w_sum[...] = jnp.zeros_like(w_sum)
    carry[...] = jnp.zeros_like(carry)
    for copy in second:
        copy.wait_recv()
    products(0, 0, 1, False)
    core0 = core_send(0)
    second1 = gather_second(1, first1)
    x0, x1, last = {}, {}, {}
    z0 = [Ring(0, 0), Ring(0, 1)]
    z1 = [Ring(1, 0), Ring(1, 1)]
    ring_x0, ring_x1 = Ring(0, 2, x0), Ring(1, 2, x1)

    def step_all(rings, s):
        for ring in rings:
            ring.step(s)

    for dz in URGENT:
        x0[dz] = core_sum(0, dz, core0)
        if dz == 4:
            step_all(z0, 0)
    step_all(z0, 1)
    ring_x0.step(0)
    for copy in second1:
        copy.wait_recv()
    products(1, 0, 2, False)
    step_all(z0, 2)
    products(1, 1, 2, False)
    core1 = core_send(1)
    step_all(z0, 3)
    ring_x0.step(1)
    for dz in URGENT:
        x1[dz] = core_sum(1, dz, core1)
        if dz == 4:
            step_all(z1, 0)
    ring_x0.step(2)
    step_all(z1, 1)
    ring_x1.step(0)
    for b in range(2):
        last[0, b] = finish_z(0, b, z0[b])
    ring_x0.step(3)
    step_all(z1, 2)
    ring_x1.step(1)
    for b in range(2):
        close_z(0, b, last[0, b])
    step_all(z1, 3)
    ring_x1.step(2)
    close_x(0, ring_x0)
    for b in range(2):
        last[1, b] = finish_z(1, b, z1[b])
    ring_x1.step(3)
    for b in range(2):
        close_z(1, b, last[1, b])
    middle(0)

    class Spread:
        def __init__(self, f, place):
            self.f, self.place = f, place
            self.up = self.down = None

        def span(self, dz, first=0, size=2):
            return grads[self.f].at[pl.ds((dz % 8) * 8 + self.place + first, size)]

        def step(self, s):
            if s > 0:
                self.done()
            first, size = ((0, 2), (1, 1))[s == 3]
            self.up = links.send(self.span(-s, 0, size), self.span(-s - 1, 0, size), z_up)
            self.down = links.send(self.span(s, first, size), self.span(s + 1, first, size), z_down)

        def done(self):
            self.up.wait_recv()
            self.down.wait_recv()

    from_twin = {0: [], 1: []}
    from_far = {}

    def to_twin(f, dz, place, size):
        at = dz * 8 + place
        from_twin[f].append(links.send(grads[f].at[pl.ds(at, size)], grads[f].at[pl.ds(64 + at, size)], twin))

    def to_far(dz, place):
        at = dz * 8 + place
        from_far[dz, place] = links.send(grads[0].at[pl.ds(at, 2)], grads[0].at[pl.ds(at + 4, 2)], x_far)

    def near(b):
        return links.send(grads[1].at[pl.ds(2 * b, 1)], grads[1].at[pl.ds(2 * b + 1, 1)], x_far)

    def around(s):
        return sorted({-s % 8, s % 8})

    late = [Spread(0, 0), Spread(0, 2)]
    early = [Spread(1, 2 * b) for b in range(4)]

    def late_round(s):
        for stream in late:
            if s < 4:
                stream.step(s)
            else:
                stream.done()
            for dz in around(s):
                to_far(dz, stream.place)
        for dz in around(s):
            to_twin(0, dz, 0, 4)

    def early_round(s):
        for b, stream in enumerate(early):
            if s == 0:
                nears[b].wait_recv()
            if s < 4:
                stream.step(s)
            else:
                stream.done()
            if b % 2:
                for dz in around(s):
                    to_twin(1, dz, 4 * (b // 2), 4)

    def far_to_twin(s):
        for dz in around(s):
            for place in (0, 2):
                from_far[dz, place].wait_recv()
            to_twin(0, dz, 4, 4)

    def all_here(f):
        for copy in from_twin[f]:
            copy.wait_recv()

    nears = [near(0), near(1)]
    late[0].step(0)
    to_far(0, 0)
    close_x(1, ring_x1)
    middle(1)
    nears += [near(2), near(3)]
    late[1].step(0)
    to_far(0, 2)
    to_twin(0, 0, 0, 4)

    def weight_start():
        def fill(i):
            for j in range(2):
                w_own[2 * i + j] = w_sum[pl.ds(8 * i, 8), j * 128 : (j + 1) * 128]

        each(32, fill)
        return links.send(w_own.at[pl.ds((1 - here["core"]) * 32, 32)], w_core.at[0], twin)

    def weight_y(copy):
        copy.wait_recv()

        def fill(i):
            w_core[1, i] = w_own[here["core"] * 32 + i] + w_core[0, i]

        each(32, fill)
        return [
            links.send(w_core.at[1, pl.ds(lax.rem(here["y"] + d, 4) * 8, 8)], w_y.at[d], y_to[d]) for d in (1, 2, 3)
        ]

    def weight_z(copies):
        for copy in copies:
            copy.wait_recv()

        def fill(i):
            w_y[0, i] = w_core[1, here["y"] * 8 + i] + w_y[1, i] + w_y[2, i] + w_y[3, i]

        each(8, fill)
        return [
            links.send(w_y.at[0, pl.ds(lax.rem(here["z"] + d, 8), 1)], w_z.at[pl.ds(d, 1)], z_to[d])
            for d in range(1, 8)
        ]

    def weight_x(copies):
        for copy in copies:
            copy.wait_recv()
        total = w_y[0, pl.ds(here["z"], 1)]
        for d in range(1, 8):
            total = total + w_z[d : d + 1]
        w_x[0:1] = total
        return [
            links.send(w_x.at[pl.ds(0, 1)], w_x.at[pl.ds(i, 1)], to)
            for i, to in ((1, x_far), (2, x_near), (3, x_both))
        ]

    def weight_all_z(copies):
        for copy in copies:
            copy.wait_recv()
        mine = pl.ds(here["z"], 1)
        w_all_z[mine] = (w_x[0:1] + w_x[1:2]) + (w_x[2:3] + w_x[3:4])
        return [links.send(w_all_z.at[mine], w_all_z.at[mine], z_to[d]) for d in range(1, 8)]

    def weight_all_y(copies):
        for copy in copies:
            copy.wait_recv()
        mine = pl.ds(here["y"] * 8, 8)

        def fill(i):
            w_all_y[here["y"] * 8 + i] = w_all_z[i]

        each(8, fill)
        return [links.send(w_all_y.at[mine], w_all_y.at[mine], y_to[d]) for d in (1, 2, 3)]

    def weight_all_core(copies):
        for copy in copies:
            copy.wait_recv()
        mine = pl.ds(here["core"] * 32, 32)

        def fill(i):
            w_all[here["core"] * 32 + i] = w_all_y[i]

        each(32, fill)
        return links.send(w_all.at[mine], w_all.at[mine], twin)

    def weight_end(copy):
        copy.wait_recv()

        def fill(i):
            for j in range(2):
                grad_weight[pl.ds(8 * i, 8), j * 128 : (j + 1) * 128] = w_all[2 * i + j]

        each(32, fill)

    def back_first(f):
        def fill(place):
            back[f, place] = slots[f, table[COL_LAST, place]]

        each(32, fill)
        near_copies = {
            d: links.send(back.at[f, pl.ds((4 + d) * 4, 2)], back_x.at[f, pl.ds(d * 2, 2)], x_near)
            for d in (2, 1, 3, 0)
        }
        y_copies = [
            links.send(back.at[f, pl.ds((x_other * 4 + d) * 4 + 2, 2)], back_y.at[f, d, pl.ds(x_other * 2, 2)], y_to[d])
            for x_other in (1, 0)
            for d in (2, 1, 3)
        ]
        return near_copies, y_copies

    def back_second(f, first):
        near_copies, y_copies = first
        y_second = []
        for d in (2, 1, 3, 0):
            near_copies[d].wait_recv()
            own = back.at[f, pl.ds(d * 4, 2)]
            add_up(own, [own, back_x.at[f, pl.ds(d * 2, 2)]])
            if d:
                y_second.append(links.send(back.at[f, pl.ds(d * 4, 2)], back_y2.at[f, d], y_to[d]))
        for copy in y_copies[:3]:
            copy.wait_recv()
        add_up(
            back_x2.at[f, pl.ds(0, 2)],
            [back.at[f, pl.ds(18, 2)]] + [back_y.at[f, d, pl.ds(2, 2)] for d in (1, 2, 3)],
        )
        near_second = links.send(back_x2.at[f, pl.ds(0, 2)], back_x2.at[f, pl.ds(2, 2)], x_near)
        return y_copies[3:], y_second, near_second

    def back_third(f, second):
        y_copies, y_second, near_second = second
        lanes = pl.ds(f * HALF, HALF)
        for copy in y_copies + [near_second]:
            copy.wait_recv()
        add_up(
            grad_feat.at[pl.ds(2, 2), :, lanes],
            [back.at[f, pl.ds(2, 2)], back_x2.at[f, pl.ds(2, 2)]]
            + [back_y.at[f, d, pl.ds(0, 2)] for d in (1, 2, 3)],
        )
        for copy in y_second:
            copy.wait_recv()
        add_up(
            grad_feat.at[pl.ds(0, 2), :, lanes],
            [back.at[f, pl.ds(0, 2)]] + [back_y2.at[f, d] for d in (1, 2, 3)],
        )

    w_copy = weight_start()
    late_round(1)
    early_round(0)
    late_round(2)
    w_copy = weight_y(w_copy)
    late_round(3)
    early_round(1)
    far_to_twin(0)
    far_to_twin(1)
    late_round(4)
    w_copy = weight_z(w_copy)
    far_to_twin(2)
    early_round(2)
    w_copy = weight_x(w_copy)
    far_to_twin(3)
    early_round(3)
    w_copy = weight_all_z(w_copy)
    far_to_twin(4)
    all_here(0)
    products(0, 0, 1, True)
    first0 = back_first(0)
    early_round(4)
    w_copy = weight_all_y(w_copy)
    all_here(1)
    products(1, 0, 2, True)
    second0 = back_second(0, first0)
    products(1, 1, 2, True)
    first1 = back_first(1)
    w_copy = weight_all_core(w_copy)
    back_third(0, second0)
    second1 = back_second(1, first1)
    weight_end(w_copy)
    back_third(1, second1)
    for copy in links.copies:
        copy.wait_send()


def finish_kernel(*refs):
    copies = [pltpu.make_async_copy(refs[i], refs[3 + i], refs[6].at[i]) for i in range(3)]
    for copy in copies:
        copy.start()
    for copy in copies:
        copy.wait()


def per_device(features, weight, cotangent, tile_rows, tile_cols, tile_values, tile_count):
    table = pl.pallas_call(
        order_kernel,
        out_shape=jax.ShapeDtypeStruct((LINES, T), jnp.int32),
        in_specs=[
            pl.BlockSpec(memory_space=pltpu.SMEM),
            pl.BlockSpec(memory_space=pltpu.VMEM),
            pl.BlockSpec(memory_space=pltpu.VMEM),
        ],
        out_specs=pl.BlockSpec(memory_space=pltpu.VMEM),
        name="order",
    )(tile_count, tile_rows.reshape(1, T), tile_cols.reshape(1, T))
    hbm, vmem = pl.BlockSpec(memory_space=pl.ANY), pl.BlockSpec(memory_space=pltpu.VMEM)

    def blocks(*counts):
        return pltpu.VMEM((*counts, T, HALF), BF16)

    def pieces(*counts):
        return pltpu.VMEM((*counts, 8, 128), F32)

    out_shape = (
        jax.ShapeDtypeStruct((4, T, 256), BF16),
        jax.ShapeDtypeStruct((4, T, 256), BF16),
        jax.ShapeDtypeStruct((256, 256), F32),
    )
    hidden, grad_feat, grad_weight = pl.pallas_call(
        layer_kernel,
        out_shape=out_shape,
        in_specs=[pl.BlockSpec(memory_space=pltpu.SMEM), hbm, vmem, hbm, hbm],
        out_specs=(vmem, vmem, vmem),
        scratch_shapes=[
            blocks(T),
            pltpu.VMEM((4, T, 256), BF16),
            blocks(32),
            blocks(32),
            blocks(2, T + 1),
            blocks(2, 64),
            blocks(2, 64),
            blocks(2, 64),
            blocks(2, 16),
            blocks(2, 3, 2, 8),
            blocks(2, 4),
            pltpu.VMEM((2, 2, T, HALF), F32),
            pltpu.VMEM((4, T, 256), BF16),
            blocks(128),
            blocks(128),
            pltpu.VMEM((T, HALF), F32),
            blocks(2, 32),
            blocks(2, 8),
            blocks(2, 4, 4),
            blocks(2, 4, 2),
            blocks(2, 4),
            pltpu.VMEM((256, 256), F32),
            pieces(64),
            pieces(2, 32),
            pieces(4, 8),
            pieces(8),
            pieces(4),
            pieces(8),
            pieces(32),
            pieces(64),
            pltpu.SemaphoreType.DMA((4,)),
            pltpu.SemaphoreType.DMA((COPIES,)),
            pltpu.SemaphoreType.DMA((COPIES,)),
        ],
        compiler_params=pltpu.CompilerParams(
            collective_id=0, has_side_effects=True, vmem_limit_bytes=60 * 2**20
        ),
        cost_estimate=pl.CostEstimate(flops=5 * 10**9, bytes_accessed=6 * 2**20, transcendentals=2**17),
        name="layer",
    )(
        table,
        features.reshape(4, T, 256),
        weight,
        cotangent.reshape(4, T, 256),
        tile_values.reshape(T, T, T),
    )
    hidden, grad_feat, grad_weight = pl.pallas_call(
        finish_kernel,
        out_shape=out_shape,
        in_specs=[hbm] * 3,
        out_specs=[vmem] * 3,
        scratch_shapes=[pltpu.SemaphoreType.DMA((3,))],
        name="finish",
    )(hidden, grad_feat, grad_weight)
    return hidden.reshape(4 * T, 256), grad_feat.reshape(4 * T, 256), grad_weight


def solution(mesh):
    placed = (
        P(("row", "col"), None),
        P(),
        P(("row", "col"), None),
        P("row", "col", None),
        P("row", "col", None),
        P("row", "col", None, None, None),
        P("row", "col"),
    )
    return jax.shard_map(
        per_device,
        mesh=mesh,
        in_specs=placed,
        out_specs=(P(("row", "col"), None), P(("row", "col"), None), P()),
        check_vma=False,
    )
```

```python
import functools

import jax
import jax.numpy as jnp
from jax import lax
from jax.experimental import pallas as pl
from jax.experimental.pallas import tpu as pltpu
from jax.sharding import PartitionSpec as P

MESH = pl.DeviceIdType.MESH
BF16 = jnp.bfloat16
F32 = jnp.float32
T = 128
HALF = 128
COPIES = 340
GROUP = 32
URGENT = (4, 3, 5, 2, 6, 1, 7, 0)


def position():
    row, col = lax.axis_index("row"), lax.axis_index("col")
    return dict(
        x_hi=col // 16, z=lax.rem(col // 2, 8), core=lax.rem(col, 2), y=row // 2, x_lo=lax.rem(row, 2)
    )


def device(here, x_hi=0, x_lo=0, y=0, z=0, core=0):
    x_hi = 1 - here["x_hi"] if x_hi else here["x_hi"]
    x_lo = 1 - here["x_lo"] if x_lo else here["x_lo"]
    core = 1 - here["core"] if core else here["core"]
    y = lax.rem(here["y"] + y, 4)
    z = lax.rem(here["z"] + z, 8)
    return (y * 2 + x_lo, x_hi * 16 + z * 2 + core)


ROW_TILE, ROW_KEEP, ROW_LAST, ROW_FEAT, COL_TILE, COL_KEEP, COL_LAST, COL_GRAD = range(8)
LINES = 16


def fill_table(here, count, rows, cols, table_ref):
    lane = lax.broadcasted_iota(jnp.int32, (T, T), 1)
    sub = lax.broadcasted_iota(jnp.int32, (T, T), 0)
    eye = lane == sub

    def spread(values):
        return jnp.broadcast_to(values, (T, T))

    def column(values):
        return jnp.broadcast_to(jnp.sum(jnp.where(eye, spread(values), 0), axis=1, keepdims=True), (T, T))

    def total(values):
        return jnp.sum(values, axis=0, keepdims=True)

    live_down = sub < count

    def feat_place(cols):
        owner = cols // 4
        return ((lax.rem(owner, 2) + here["x_lo"]) % 2 * 4 + (owner // 2 - here["y"] + 4) % 4) * 4 + lax.rem(cols, 4)

    def row_place(rows, order):
        owner, block = rows // 4, lax.rem(rows, 4)
        x_other = (owner // 16 + here["x_hi"]) % 2
        z_away = (lax.rem(owner // 2, 8) - here["z"] + 8) % 8
        core_other = (lax.rem(owner, 2) + here["core"]) % 2
        return (core_other * 8 + z_away) * 8 + order(block, x_other)

    def sum_order(block, x_other):
        return jnp.where(block < 2, 2 * block + x_other, 2 + block + 2 * x_other)

    def far_last(block, x_other):
        return block + 4 * x_other

    def far_first(block, x_other):
        return 2 * block + x_other

    rows_down, cols_down = column(rows), feat_place(column(cols))
    grads_down = [row_place(rows_down, far_last), row_place(rows_down, far_first)]
    rows_down = row_place(rows_down, sum_order)
    rows, cols = row_place(rows, sum_order), feat_place(cols)

    def sorted_by(keys, keys_down, values_down):
        big = T * T
        key = jnp.where(lane < count, spread(keys) * T + lane, big + lane)
        key_down = jnp.where(live_down, keys_down * T + sub, big + sub)
        rank_down = jnp.sum(jnp.where(key < key_down, 1, 0), axis=1, keepdims=True)
        rank_down = jnp.broadcast_to(rank_down, (T, T))
        now = rank_down == lane
        tile = total(jnp.where(now, sub, 0))
        values = [total(jnp.where(now, value, 0)) for value in values_down]
        mine = total(jnp.where(now, keys_down, 0))
        before = total(jnp.where(rank_down == lane - 1, keys_down, 0))
        first = lax.broadcasted_iota(jnp.int32, (1, T), 1) == 0
        keep = jnp.where(jnp.logical_or(first, mine != before), 0, 1)
        upto = total(jnp.where(jnp.logical_and(live_down, keys_down <= lane), 1, 0))
        some = total(jnp.where(jnp.logical_and(live_down, keys_down == lane), 1, 0))
        return [tile, keep, jnp.where(some > 0, upto - 1, T), *values]

    lines = sorted_by(rows, rows_down, [cols_down]) + sorted_by(cols, cols_down, grads_down)
    table_ref[...] = jnp.zeros_like(table_ref)
    for number, line in enumerate(lines):
        table_ref[number : number + 1, :] = line


def each(count, body):
    def step(i, carried):
        body(i)
        return carried

    lax.fori_loop(0, count, step, 0)


def add_up(out, terms):
    def body(i):
        rows = pl.ds(i * 32, 32)
        total = terms[0][:, rows].astype(F32)
        for term in terms[1:]:
            total = total + term[:, rows].astype(F32)
        out[:, rows] = total.astype(out.dtype)

    each(T // 32, body)


class Links:
    def __init__(self, send_sem, recv_sem):
        self.send_sem, self.recv_sem, self.copies = send_sem, recv_sem, []

    def send(self, src, dst, to):
        number = len(self.copies)
        copy = pltpu.make_async_remote_copy(
            src_ref=src,
            dst_ref=dst,
            send_sem=self.send_sem.at[number],
            recv_sem=self.recv_sem.at[number],
            device_id=to,
            device_id_type=MESH,
        )
        copy.start()
        self.copies.append(copy)
        return copy


def layer_kernel(
    count,
    rows_hbm,
    cols_hbm,
    feat_hbm,
    weight_hbm,
    cot_hbm,
    tile_hbm,
    hidden,
    grad_feat,
    grad_weight,
    table,
    lines,
    rows_in,
    cols_in,
    weight,
    tiles,
    cot,
    feats0,
    feats1,
    slots,
    give,
    core_in,
    value,
    x_in,
    ring_in,
    x_last,
    part,
    summed,
    grads0,
    grads1,
    carry,
    back,
    back_x,
    back_y,
    back_y2,
    back_x2,
    w_sum,
    w_own,
    w_core,
    w_y,
    w_z,
    w_x,
    w_all_z,
    w_all_y,
    w_all,
    local_sem,
    send_sem,
    recv_sem,
):
    here = position()
    feats, grads = (feats0, feats1), (grads0, grads1)
    links = Links(send_sem, recv_sem)
    z_up, z_down = device(here, z=1), device(here, z=7)
    x_far, x_near = device(here, x_hi=1), device(here, x_lo=1)
    x_both = device(here, x_hi=1, x_lo=1)
    twin = device(here, core=1)
    y_to = {d: device(here, y=d) for d in (1, 2, 3)}
    z_to = {d: device(here, z=d) for d in range(1, 8)}

    feat_own = [feat_hbm.at[:, :, pl.ds(f * HALF, HALF)] for f in range(2)]
    moves = [
        (rows_hbm, rows_in),
        (cols_hbm, cols_in),
        (feat_own[0], feats[0].at[pl.ds(0, 4)]),
        (feat_own[1], feats[1].at[pl.ds(0, 4)]),
        (tile_hbm, tiles),
        (weight_hbm, weight),
        (cot_hbm, cot),
    ]
    loads = [pltpu.make_async_copy(src, dst, local_sem.at[i]) for i, (src, dst) in enumerate(moves)]
    for load in loads:
        load.start()

    barrier = pltpu.get_barrier_semaphore()
    partners = [x_far, x_near, twin, z_up, z_down, *y_to.values()]
    for partner in partners:
        pl.semaphore_signal(barrier, inc=1, device_id=partner, device_id_type=MESH)
    pl.semaphore_wait(barrier, len(partners))

    def gather_first(f):
        own = feat_own[f]
        near = links.send(own, feats[f].at[pl.ds(16, 4)], x_near)
        over = {d: links.send(own, feats[f].at[pl.ds((4 - d) * 4, 4)], y_to[d]) for d in (1, 3, 2)}
        return near, over

    def gather_second(f, first):
        near, over = first
        near.wait_recv()
        copies = [
            links.send(feats[f].at[pl.ds(16, 2)], feats[f].at[pl.ds(16 + (4 - d) * 4, 2)], y_to[d])
            for d in (1, 3, 2)
        ]
        for d in (1, 3, 2):
            over[d].wait_recv()
            rows = (4 - d) * 4 + 2
            copies.append(links.send(feats[f].at[pl.ds(rows, 2)], feats[f].at[pl.ds(16 + rows, 2)], x_near))
        return copies

    def products(f, piece, pieces, back_pass):
        tile_line, value_line, keep_line = (
            (COL_TILE, COL_GRAD + f, COL_KEEP) if back_pass else (ROW_TILE, ROW_FEAT, ROW_KEEP)
        )
        steps = T // GROUP // pieces
        source = (grads if back_pass else feats)[f]

        def step(i):
            total = carry[...]
            for u in range(GROUP):
                t = i * GROUP + u
                tile = tiles[table[tile_line, t]]
                block = source[table[value_line, t]]
                if back_pass:
                    tile = tile.T
                term = jnp.dot(tile, block, preferred_element_type=F32)
                total = term + total * table[keep_line, t].astype(F32)
                slots[f, t] = total.astype(BF16)
            carry[...] = total

        each(steps, lambda i: step(piece * steps + i))

    def core_send(f):
        copies = {}
        for dz in URGENT:

            def fill(place, dz=dz):
                give[f, dz * 8 + place] = slots[f, table[ROW_LAST, 64 + dz * 8 + place]]

            each(8, fill)
            span = pl.ds(dz * 8, 8)
            copies[dz] = links.send(give.at[f, span], core_in.at[f, span], twin)
        return copies

    def core_sum(f, dz, copies):
        copies[dz].wait_recv()

        def fill(place):
            at = dz * 8 + place
            own = slots[f, table[ROW_LAST, at]].astype(F32)
            value[f, at] = (own + core_in[f, at].astype(F32)).astype(BF16)

        each(8, fill)
        return links.send(value.at[f, pl.ds(dz * 8 + 6, 2)], x_in.at[f, pl.ds(dz * 2, 2)], x_far)

    class Ring:
        def __init__(self, f, stream, x_copies=None):
            self.f, self.stream, self.x_copies = f, stream, x_copies
            self.up = self.down = None

        def span(self, dz, first=0, size=2):
            return value.at[self.f, pl.ds(dz * 8 + self.stream * 2 + first, size)]

        def own(self, dz, first=0, size=2):
            if self.x_copies is None:
                return [self.span(dz, first, size)]
            return [self.span(dz, first, size), x_in.at[self.f, pl.ds(dz * 2 + first, size)]]

        def slot(self, way, step, first=0, size=2):
            return ring_in.at[self.f, self.stream, way, pl.ds(step * 2 + first, size)]

        def step(self, s):
            if s == 0:
                if self.x_copies is not None:
                    self.x_copies[4].wait_recv()
                    add_up(self.span(4), self.own(4))
                self.up = links.send(self.span(4, 0, 1), self.slot(0, 0, 0, 1), z_up)
                self.down = links.send(self.span(4, 1, 1), self.slot(1, 0, 1, 1), z_down)
                return
            for way, dz in ((0, 4 - s), (1, 4 + s)):
                if self.x_copies is not None:
                    self.x_copies[dz].wait_recv()
                (self.up, self.down)[way].wait_recv()
                if s == 1:
                    add_up(self.span(dz, way, 1), self.own(dz, way, 1) + [self.slot(way, 0, way, 1)])
                    if self.x_copies is not None:
                        add_up(self.span(dz, 1 - way, 1), self.own(dz, 1 - way, 1))
                else:
                    add_up(self.span(dz), self.own(dz) + [self.slot(way, s - 1)])
                sent = links.send(self.span(dz), self.slot(way, s), (z_up, z_down)[way])
                if way == 0:
                    self.up = sent
                else:
                    self.down = sent

        def finish(self):
            if self.x_copies is not None:
                self.x_copies[0].wait_recv()
            self.up.wait_recv()
            self.down.wait_recv()

        def last(self, first, size):
            return self.own(0, first, size) + [self.slot(0, 3, first, size), self.slot(1, 3, first, size)]

    def finish_z(f, b, ring):
        ring.finish()
        far = pl.ds(2 * f + b, 1)
        add_up(x_last.at[0, far], ring.last(1, 1))
        copy = links.send(x_last.at[0, far], x_last.at[1, far], x_far)
        add_up(part.at[f, pl.ds(b, 1)], ring.last(0, 1))
        return copy

    def close_z(f, b, copy):
        copy.wait_recv()
        add_up(
            summed.at[pl.ds(b, 1), :, pl.ds(f * HALF, HALF)],
            [part.at[f, pl.ds(b, 1)], x_last.at[1, pl.ds(2 * f + b, 1)]],
        )

    def close_x(f, ring):
        ring.finish()
        add_up(summed.at[pl.ds(2, 2), :, pl.ds(f * HALF, HALF)], ring.last(0, 2))

    def middle(pair):
        def body(i):
            b = 2 * pair + i
            rows = summed[b]
            pre = jnp.dot(rows, weight[...], preferred_element_type=F32)
            sig = jax.nn.sigmoid(pre)
            hidden[b] = (pre * sig).astype(BF16)
            grad_pre = (cot[b].astype(F32) * sig * (1.0 + pre * (1.0 - sig))).astype(BF16)
            own = lax.dot_general(
                grad_pre, weight[...], (((1,), (1,)), ((), ())), preferred_element_type=F32
            )
            grads[0][b] = own[:, :HALF].astype(BF16)
            grads[1][2 * b] = own[:, HALF:].astype(BF16)
            w_sum[...] += jnp.dot(rows.T, grad_pre, preferred_element_type=F32)

        each(2, body)

    first = gather_first(0)
    loads[0].wait()
    loads[1].wait()
    fill_table(here, count[0, 0], rows_in[...], cols_in[...], lines)
    table_copy = pltpu.make_async_copy(lines, table, local_sem.at[7])
    table_copy.start()
    for load in loads[2:]:
        load.wait()
    second = gather_second(0, first)
    first1 = gather_first(1)
    table_copy.wait()
    for f in range(2):
        slots[f, T] = jnp.zeros((T, HALF), BF16)
    w_sum[...] = jnp.zeros_like(w_sum)
    carry[...] = jnp.zeros_like(carry)
    for copy in second:
        copy.wait_recv()
    products(0, 0, 1, False)
    core0 = core_send(0)
    second1 = gather_second(1, first1)
    x0, x1, last = {}, {}, {}
    z0 = [Ring(0, 0), Ring(0, 1)]
    z1 = [Ring(1, 0), Ring(1, 1)]
    ring_x0, ring_x1 = Ring(0, 2, x0), Ring(1, 2, x1)

    def step_all(rings, s):
        for ring in rings:
            ring.step(s)

    for dz in URGENT:
        x0[dz] = core_sum(0, dz, core0)
        if dz == 4:
            step_all(z0, 0)
    step_all(z0, 1)
    ring_x0.step(0)
    for copy in second1:
        copy.wait_recv()
    products(1, 0, 2, False)
    step_all(z0, 2)
    products(1, 1, 2, False)
    core1 = core_send(1)
    step_all(z0, 3)
    ring_x0.step(1)
    for dz in URGENT:
        x1[dz] = core_sum(1, dz, core1)
        if dz == 4:
            step_all(z1, 0)
    ring_x0.step(2)
    step_all(z1, 1)
    ring_x1.step(0)
    for b in range(2):
        last[0, b] = finish_z(0, b, z0[b])
    ring_x0.step(3)
    step_all(z1, 2)
    ring_x1.step(1)
    for b in range(2):
        close_z(0, b, last[0, b])
    step_all(z1, 3)
    ring_x1.step(2)
    close_x(0, ring_x0)
    for b in range(2):
        last[1, b] = finish_z(1, b, z1[b])
    ring_x1.step(3)
    for b in range(2):
        close_z(1, b, last[1, b])
    middle(0)

    class Spread:
        def __init__(self, f, place):
            self.f, self.place = f, place
            self.up = self.down = None

        def span(self, dz, first=0, size=2):
            return grads[self.f].at[pl.ds((dz % 8) * 8 + self.place + first, size)]

        def step(self, s):
            if s > 0:
                self.done()
            first, size = ((0, 2), (1, 1))[s == 3]
            self.up = links.send(self.span(-s, 0, size), self.span(-s - 1, 0, size), z_up)
            self.down = links.send(self.span(s, first, size), self.span(s + 1, first, size), z_down)

        def done(self):
            self.up.wait_recv()
            self.down.wait_recv()

    from_twin = {0: [], 1: []}
    from_far = {}

    def to_twin(f, dz, place, size):
        at = dz * 8 + place
        from_twin[f].append(links.send(grads[f].at[pl.ds(at, size)], grads[f].at[pl.ds(64 + at, size)], twin))

    def to_far(dz, place):
        at = dz * 8 + place
        from_far[dz, place] = links.send(grads[0].at[pl.ds(at, 2)], grads[0].at[pl.ds(at + 4, 2)], x_far)

    def near(b):
        return links.send(grads[1].at[pl.ds(2 * b, 1)], grads[1].at[pl.ds(2 * b + 1, 1)], x_far)

    def around(s):
        return sorted({-s % 8, s % 8})

    late = [Spread(0, 0), Spread(0, 2)]
    early = [Spread(1, 2 * b) for b in range(4)]

    def late_round(s):
        for stream in late:
            if s < 4:
                stream.step(s)
            else:
                stream.done()
            for dz in around(s):
                to_far(dz, stream.place)
        for dz in around(s):
            to_twin(0, dz, 0, 4)

    def early_round(s):
        for b, stream in enumerate(early):
            if s == 0:
                nears[b].wait_recv()
            if s < 4:
                stream.step(s)
            else:
                stream.done()
            if b % 2:
                for dz in around(s):
                    to_twin(1, dz, 4 * (b // 2), 4)

    def far_to_twin(s):
        for dz in around(s):
            for place in (0, 2):
                from_far[dz, place].wait_recv()
            to_twin(0, dz, 4, 4)

    def all_here(f):
        for copy in from_twin[f]:
            copy.wait_recv()

    nears = [near(0), near(1)]
    late[0].step(0)
    to_far(0, 0)
    close_x(1, ring_x1)
    middle(1)
    nears += [near(2), near(3)]
    late[1].step(0)
    to_far(0, 2)
    to_twin(0, 0, 0, 4)

    def weight_start():
        def fill(i):
            for j in range(2):
                w_own[2 * i + j] = w_sum[pl.ds(8 * i, 8), j * 128 : (j + 1) * 128]

        each(32, fill)
        return links.send(w_own.at[pl.ds((1 - here["core"]) * 32, 32)], w_core.at[0], twin)

    def weight_y(copy):
        copy.wait_recv()

        def fill(i):
            w_core[1, i] = w_own[here["core"] * 32 + i] + w_core[0, i]

        each(32, fill)
        return [
            links.send(w_core.at[1, pl.ds(lax.rem(here["y"] + d, 4) * 8, 8)], w_y.at[d], y_to[d]) for d in (1, 2, 3)
        ]

    def weight_z(copies):
        for copy in copies:
            copy.wait_recv()

        def fill(i):
            w_y[0, i] = w_core[1, here["y"] * 8 + i] + w_y[1, i] + w_y[2, i] + w_y[3, i]

        each(8, fill)
        return [
            links.send(w_y.at[0, pl.ds(lax.rem(here["z"] + d, 8), 1)], w_z.at[pl.ds(d, 1)], z_to[d])
            for d in range(1, 8)
        ]

    def weight_x(copies):
        for copy in copies:
            copy.wait_recv()
        total = w_y[0, pl.ds(here["z"], 1)]
        for d in range(1, 8):
            total = total + w_z[d : d + 1]
        w_x[0:1] = total
        return [
            links.send(w_x.at[pl.ds(0, 1)], w_x.at[pl.ds(i, 1)], to)
            for i, to in ((1, x_far), (2, x_near), (3, x_both))
        ]

    def weight_all_z(copies):
        for copy in copies:
            copy.wait_recv()
        mine = pl.ds(here["z"], 1)
        w_all_z[mine] = (w_x[0:1] + w_x[1:2]) + (w_x[2:3] + w_x[3:4])
        return [links.send(w_all_z.at[mine], w_all_z.at[mine], z_to[d]) for d in range(1, 8)]

    def weight_all_y(copies):
        for copy in copies:
            copy.wait_recv()
        mine = pl.ds(here["y"] * 8, 8)

        def fill(i):
            w_all_y[here["y"] * 8 + i] = w_all_z[i]

        each(8, fill)
        return [links.send(w_all_y.at[mine], w_all_y.at[mine], y_to[d]) for d in (1, 2, 3)]

    def weight_all_core(copies):
        for copy in copies:
            copy.wait_recv()
        mine = pl.ds(here["core"] * 32, 32)

        def fill(i):
            w_all[here["core"] * 32 + i] = w_all_y[i]

        each(32, fill)
        return links.send(w_all.at[mine], w_all.at[mine], twin)

    def weight_end(copy):
        copy.wait_recv()

        def fill(i):
            for j in range(2):
                grad_weight[pl.ds(8 * i, 8), j * 128 : (j + 1) * 128] = w_all[2 * i + j]

        each(32, fill)

    def back_first(f):
        def fill(place):
            back[f, place] = slots[f, table[COL_LAST, place]]

        each(32, fill)
        near_copies = {
            d: links.send(back.at[f, pl.ds((4 + d) * 4, 2)], back_x.at[f, pl.ds(d * 2, 2)], x_near)
            for d in (2, 1, 3, 0)
        }
        y_copies = [
            links.send(back.at[f, pl.ds((x_other * 4 + d) * 4 + 2, 2)], back_y.at[f, d, pl.ds(x_other * 2, 2)], y_to[d])
            for x_other in (1, 0)
            for d in (2, 1, 3)
        ]
        return near_copies, y_copies

    def back_second(f, first):
        near_copies, y_copies = first
        y_second = []
        for d in (2, 1, 3, 0):
            near_copies[d].wait_recv()
            own = back.at[f, pl.ds(d * 4, 2)]
            add_up(own, [own, back_x.at[f, pl.ds(d * 2, 2)]])
            if d:
                y_second.append(links.send(back.at[f, pl.ds(d * 4, 2)], back_y2.at[f, d], y_to[d]))
        for copy in y_copies[:3]:
            copy.wait_recv()
        add_up(
            back_x2.at[f, pl.ds(0, 2)],
            [back.at[f, pl.ds(18, 2)]] + [back_y.at[f, d, pl.ds(2, 2)] for d in (1, 2, 3)],
        )
        near_second = links.send(back_x2.at[f, pl.ds(0, 2)], back_x2.at[f, pl.ds(2, 2)], x_near)
        return y_copies[3:], y_second, near_second

    def back_third(f, second):
        y_copies, y_second, near_second = second
        lanes = pl.ds(f * HALF, HALF)
        for copy in y_copies + [near_second]:
            copy.wait_recv()
        add_up(
            grad_feat.at[pl.ds(2, 2), :, lanes],
            [back.at[f, pl.ds(2, 2)], back_x2.at[f, pl.ds(2, 2)]]
            + [back_y.at[f, d, pl.ds(0, 2)] for d in (1, 2, 3)],
        )
        for copy in y_second:
            copy.wait_recv()
        add_up(
            grad_feat.at[pl.ds(0, 2), :, lanes],
            [back.at[f, pl.ds(0, 2)]] + [back_y2.at[f, d] for d in (1, 2, 3)],
        )

    w_copy = weight_start()
    late_round(1)
    early_round(0)
    late_round(2)
    w_copy = weight_y(w_copy)
    late_round(3)
    early_round(1)
    far_to_twin(0)
    far_to_twin(1)
    late_round(4)
    w_copy = weight_z(w_copy)
    far_to_twin(2)
    early_round(2)
    w_copy = weight_x(w_copy)
    far_to_twin(3)
    early_round(3)
    w_copy = weight_all_z(w_copy)
    far_to_twin(4)
    all_here(0)
    products(0, 0, 1, True)
    first0 = back_first(0)
    early_round(4)
    w_copy = weight_all_y(w_copy)
    all_here(1)
    products(1, 0, 2, True)
    second0 = back_second(0, first0)
    products(1, 1, 2, True)
    first1 = back_first(1)
    w_copy = weight_all_core(w_copy)
    back_third(0, second0)
    second1 = back_second(1, first1)
    weight_end(w_copy)
    back_third(1, second1)
    for copy in links.copies:
        copy.wait_send()


def finish_kernel(*refs):
    copies = [pltpu.make_async_copy(refs[i], refs[3 + i], refs[6].at[i]) for i in range(3)]
    for copy in copies:
        copy.start()
    for copy in copies:
        copy.wait()


def per_device(features, weight, cotangent, tile_rows, tile_cols, tile_values, tile_count):
    hbm, vmem = pl.BlockSpec(memory_space=pl.ANY), pl.BlockSpec(memory_space=pltpu.VMEM)

    def blocks(*counts):
        return pltpu.VMEM((*counts, T, HALF), BF16)

    def pieces(*counts):
        return pltpu.VMEM((*counts, 8, 128), F32)

    out_shape = (
        jax.ShapeDtypeStruct((4, T, 256), BF16),
        jax.ShapeDtypeStruct((4, T, 256), BF16),
        jax.ShapeDtypeStruct((256, 256), F32),
    )
    hidden, grad_feat, grad_weight = pl.pallas_call(
        layer_kernel,
        out_shape=out_shape,
        in_specs=[pl.BlockSpec(memory_space=pltpu.SMEM)] + [hbm] * 6,
        out_specs=(vmem, vmem, vmem),
        scratch_shapes=[
            pltpu.SMEM((LINES, T), jnp.int32),
            pltpu.VMEM((LINES, T), jnp.int32),
            pltpu.VMEM((1, T), jnp.int32),
            pltpu.VMEM((1, T), jnp.int32),
            pltpu.VMEM((256, 256), BF16),
            blocks(T),
            pltpu.VMEM((4, T, 256), BF16),
            blocks(32),
            blocks(32),
            blocks(2, T + 1),
            blocks(2, 64),
            blocks(2, 64),
            blocks(2, 64),
            blocks(2, 16),
            blocks(2, 3, 2, 8),
            blocks(2, 4),
            pltpu.VMEM((2, 2, T, HALF), F32),
            pltpu.VMEM((4, T, 256), BF16),
            blocks(128),
            blocks(128),
            pltpu.VMEM((T, HALF), F32),
            blocks(2, 32),
            blocks(2, 8),
            blocks(2, 4, 4),
            blocks(2, 4, 2),
            blocks(2, 4),
            pltpu.VMEM((256, 256), F32),
            pieces(64),
            pieces(2, 32),
            pieces(4, 8),
            pieces(8),
            pieces(4),
            pieces(8),
            pieces(32),
            pieces(64),
            pltpu.SemaphoreType.DMA((8,)),
            pltpu.SemaphoreType.DMA((COPIES,)),
            pltpu.SemaphoreType.DMA((COPIES,)),
        ],
        compiler_params=pltpu.CompilerParams(
            collective_id=0, has_side_effects=True, vmem_limit_bytes=60 * 2**20
        ),
        cost_estimate=pl.CostEstimate(flops=5 * 10**9, bytes_accessed=6 * 2**20, transcendentals=2**17),
        name="layer",
    )(
        tile_count,
        tile_rows.reshape(1, T),
        tile_cols.reshape(1, T),
        features.reshape(4, T, 256),
        weight,
        cotangent.reshape(4, T, 256),
        tile_values.reshape(T, T, T),
    )
    hidden, grad_feat, grad_weight = pl.pallas_call(
        finish_kernel,
        out_shape=out_shape,
        in_specs=[hbm] * 3,
        out_specs=[vmem] * 3,
        scratch_shapes=[pltpu.SemaphoreType.DMA((3,))],
        name="finish",
    )(hidden, grad_feat, grad_weight)
    return hidden.reshape(4 * T, 256), grad_feat.reshape(4 * T, 256), grad_weight


def solution(mesh):
    placed = (
        P(("row", "col"), None),
        P(),
        P(("row", "col"), None),
        P("row", "col", None),
        P("row", "col", None),
        P("row", "col", None, None, None),
        P("row", "col"),
    )
    return jax.shard_map(
        per_device,
        mesh=mesh,
        in_specs=placed,
        out_specs=(P(("row", "col"), None), P(("row", "col"), None), P()),
        check_vma=False,
    )
```

```python
import functools

import jax
import jax.numpy as jnp
from jax import lax
from jax.experimental import pallas as pl
from jax.experimental.pallas import tpu as pltpu
from jax.sharding import PartitionSpec as P

MESH = pl.DeviceIdType.MESH
BF16 = jnp.bfloat16
F32 = jnp.float32
T = 128
HALF = 128
COPIES = 340
GROUP = 32
URGENT = (4, 3, 5, 2, 6, 1, 7, 0)


def position():
    row, col = lax.axis_index("row"), lax.axis_index("col")
    return dict(
        x_hi=col // 16, z=lax.rem(col // 2, 8), core=lax.rem(col, 2), y=row // 2, x_lo=lax.rem(row, 2)
    )


def device(here, x_hi=0, x_lo=0, y=0, z=0, core=0):
    x_hi = 1 - here["x_hi"] if x_hi else here["x_hi"]
    x_lo = 1 - here["x_lo"] if x_lo else here["x_lo"]
    core = 1 - here["core"] if core else here["core"]
    y = lax.rem(here["y"] + y, 4)
    z = lax.rem(here["z"] + z, 8)
    return (y * 2 + x_lo, x_hi * 16 + z * 2 + core)


ROW_TILE, ROW_KEEP, ROW_LAST, ROW_FEAT, COL_TILE, COL_KEEP, COL_LAST, COL_GRAD = range(8)
LINES = 16


def fill_table(here, count, rows, cols, table_ref):
    lane = lax.broadcasted_iota(jnp.int32, (T, T), 1)
    sub = lax.broadcasted_iota(jnp.int32, (T, T), 0)
    eye = lane == sub

    def spread(values):
        return jnp.broadcast_to(values, (T, T))

    def column(values):
        return jnp.broadcast_to(jnp.sum(jnp.where(eye, spread(values), 0), axis=1, keepdims=True), (T, T))

    def total(values):
        return jnp.sum(values, axis=0, keepdims=True)

    live_down = sub < count

    def feat_place(cols):
        owner = cols // 4
        return ((lax.rem(owner, 2) + here["x_lo"]) % 2 * 4 + (owner // 2 - here["y"] + 4) % 4) * 4 + lax.rem(cols, 4)

    def row_place(rows, order):
        owner, block = rows // 4, lax.rem(rows, 4)
        x_other = (owner // 16 + here["x_hi"]) % 2
        z_away = (lax.rem(owner // 2, 8) - here["z"] + 8) % 8
        core_other = (lax.rem(owner, 2) + here["core"]) % 2
        return (core_other * 8 + z_away) * 8 + order(block, x_other)

    def sum_order(block, x_other):
        return jnp.where(block < 2, 2 * block + x_other, 2 + block + 2 * x_other)

    def far_last(block, x_other):
        return block + 4 * x_other

    def far_first(block, x_other):
        return 2 * block + x_other

    rows_down, cols_down = column(rows), feat_place(column(cols))
    grads_down = [row_place(rows_down, far_last), row_place(rows_down, far_first)]
    rows_down = row_place(rows_down, sum_order)
    rows, cols = row_place(rows, sum_order), feat_place(cols)

    def sorted_by(keys, keys_down, values_down):
        big = T * T
        key = jnp.where(lane < count, spread(keys) * T + lane, big + lane)
        key_down = jnp.where(live_down, keys_down * T + sub, big + sub)
        rank_down = jnp.sum(jnp.where(key < key_down, 1, 0), axis=1, keepdims=True)
        rank_down = jnp.broadcast_to(rank_down, (T, T))
        now = rank_down == lane
        tile = total(jnp.where(now, sub, 0))
        values = [total(jnp.where(now, value, 0)) for value in values_down]
        mine = total(jnp.where(now, keys_down, 0))
        before = total(jnp.where(rank_down == lane - 1, keys_down, 0))
        first = lax.broadcasted_iota(jnp.int32, (1, T), 1) == 0
        keep = jnp.where(jnp.logical_or(first, mine != before), 0, 1)
        upto = total(jnp.where(jnp.logical_and(live_down, keys_down <= lane), 1, 0))
        some = total(jnp.where(jnp.logical_and(live_down, keys_down == lane), 1, 0))
        return [tile, keep, jnp.where(some > 0, upto - 1, T), *values]

    lines = sorted_by(rows, rows_down, [cols_down]) + sorted_by(cols, cols_down, grads_down)
    table_ref[...] = jnp.zeros_like(table_ref)
    for number, line in enumerate(lines):
        table_ref[number : number + 1, :] = line


def each(count, body):
    def step(i, carried):
        body(i)
        return carried

    lax.fori_loop(0, count, step, 0)


def add_up(out, terms):
    def body(i):
        rows = pl.ds(i * 32, 32)
        total = terms[0][:, rows].astype(F32)
        for term in terms[1:]:
            total = total + term[:, rows].astype(F32)
        out[:, rows] = total.astype(out.dtype)

    each(T // 32, body)


class Links:
    def __init__(self, send_sem, recv_sem):
        self.send_sem, self.recv_sem, self.copies = send_sem, recv_sem, []

    def send(self, src, dst, to):
        number = len(self.copies)
        copy = pltpu.make_async_remote_copy(
            src_ref=src,
            dst_ref=dst,
            send_sem=self.send_sem.at[number],
            recv_sem=self.recv_sem.at[number],
            device_id=to,
            device_id_type=MESH,
        )
        copy.start()
        self.copies.append(copy)
        return copy


def layer_kernel(
    count_hbm,
    rows_hbm,
    cols_hbm,
    feat_hbm,
    weight_hbm,
    cot_hbm,
    tile_hbm,
    hidden,
    grad_feat,
    grad_weight,
    table,
    lines,
    count,
    rows_in,
    cols_in,
    weight,
    tiles,
    cot,
    feats0,
    feats1,
    slots,
    give,
    core_in,
    value,
    x_in,
    ring_in,
    x_last,
    part,
    summed,
    grads0,
    grads1,
    carry,
    back,
    back_x,
    back_y,
    back_y2,
    back_x2,
    w_sum,
    w_own,
    w_core,
    w_y,
    w_z,
    w_x,
    w_all_z,
    w_all_y,
    w_all,
    local_sem,
    send_sem,
    recv_sem,
):
    here = position()
    feats, grads = (feats0, feats1), (grads0, grads1)
    links = Links(send_sem, recv_sem)
    z_up, z_down = device(here, z=1), device(here, z=7)
    x_far, x_near = device(here, x_hi=1), device(here, x_lo=1)
    x_both = device(here, x_hi=1, x_lo=1)
    twin = device(here, core=1)
    y_to = {d: device(here, y=d) for d in (1, 2, 3)}
    z_to = {d: device(here, z=d) for d in range(1, 8)}

    feat_own = [feat_hbm.at[:, :, pl.ds(f * HALF, HALF)] for f in range(2)]
    moves = [
        (rows_hbm, rows_in),
        (cols_hbm, cols_in),
        (feat_own[0], feats[0].at[pl.ds(0, 4)]),
        (feat_own[1], feats[1].at[pl.ds(0, 4)]),
        (tile_hbm, tiles),
        (weight_hbm, weight),
        (cot_hbm, cot),
        (count_hbm, count),
    ]
    loads = [pltpu.make_async_copy(src, dst, local_sem.at[i]) for i, (src, dst) in enumerate(moves)]
    for load in loads:
        load.start()

    barrier = pltpu.get_barrier_semaphore()
    partners = [x_far, x_near, twin, z_up, z_down, *y_to.values()]
    for partner in partners:
        pl.semaphore_signal(barrier, inc=1, device_id=partner, device_id_type=MESH)
    pl.semaphore_wait(barrier, len(partners))

    def gather_first(f):
        own = [feat_own[f].at[pl.ds(b, 2)] for b in (0, 2)]
        near = [links.send(own[i], feats[f].at[pl.ds(16 + 2 * i, 2)], x_near) for i in range(2)]
        over = [
            {d: links.send(own[i], feats[f].at[pl.ds((4 - d) * 4 + 2 * i, 2)], y_to[d]) for d in (2, 1, 3)}
            for i in (1, 0)
        ]
        return near, over

    def gather_y(f, first):
        near, _ = first
        size = 4 if f else 2
        near[0].wait_recv()
        if f:
            near[1].wait_recv()
        return [
            links.send(feats[f].at[pl.ds(16, size)], feats[f].at[pl.ds(16 + (4 - d) * 4, size)], y_to[d])
            for d in (2, 1, 3)
        ]

    def gather_x(f, first):
        near, (late_over, over) = first
        copies = [near[1], *over.values()]
        for d in (1, 3, 2):
            late_over[d].wait_recv()
            rows = (4 - d) * 4 + 2
            copies.append(links.send(feats[f].at[pl.ds(rows, 2)], feats[f].at[pl.ds(16 + rows, 2)], x_near))
        return copies

    def products(f, piece, pieces, back_pass):
        tile_line, value_line, keep_line = (
            (COL_TILE, COL_GRAD + f, COL_KEEP) if back_pass else (ROW_TILE, ROW_FEAT, ROW_KEEP)
        )
        steps = T // GROUP // pieces
        source = (grads if back_pass else feats)[f]

        def step(i):
            total = carry[...]
            for u in range(GROUP):
                t = i * GROUP + u
                tile = tiles[table[tile_line, t]]
                block = source[table[value_line, t]]
                if back_pass:
                    tile = tile.T
                term = jnp.dot(tile, block, preferred_element_type=F32)
                total = term + total * table[keep_line, t].astype(F32)
                slots[f, t] = total.astype(BF16)
            carry[...] = total

        each(steps, lambda i: step(piece * steps + i))

    def core_send(f):
        copies = {}
        for dz in URGENT:

            def fill(place, dz=dz):
                give[f, dz * 8 + place] = slots[f, table[ROW_LAST, 64 + dz * 8 + place]]

            each(8, fill)
            span = pl.ds(dz * 8, 8)
            copies[dz] = links.send(give.at[f, span], core_in.at[f, span], twin)
        return copies

    def core_sum(f, dz, copies):
        copies[dz].wait_recv()

        def fill(place):
            at = dz * 8 + place
            own = slots[f, table[ROW_LAST, at]].astype(F32)
            value[f, at] = (own + core_in[f, at].astype(F32)).astype(BF16)

        each(8, fill)
        return links.send(value.at[f, pl.ds(dz * 8 + 6, 2)], x_in.at[f, pl.ds(dz * 2, 2)], x_far)

    class Ring:
        def __init__(self, f, stream, x_copies=None):
            self.f, self.stream, self.x_copies = f, stream, x_copies
            self.up = self.down = None

        def span(self, dz, first=0, size=2):
            return value.at[self.f, pl.ds(dz * 8 + self.stream * 2 + first, size)]

        def own(self, dz, first=0, size=2):
            if self.x_copies is None:
                return [self.span(dz, first, size)]
            return [self.span(dz, first, size), x_in.at[self.f, pl.ds(dz * 2 + first, size)]]

        def slot(self, way, step, first=0, size=2):
            return ring_in.at[self.f, self.stream, way, pl.ds(step * 2 + first, size)]

        def step(self, s):
            if s == 0:
                if self.x_copies is not None:
                    self.x_copies[4].wait_recv()
                    add_up(self.span(4), self.own(4))
                self.up = links.send(self.span(4, 0, 1), self.slot(0, 0, 0, 1), z_up)
                self.down = links.send(self.span(4, 1, 1), self.slot(1, 0, 1, 1), z_down)
                return
            for way, dz in ((0, 4 - s), (1, 4 + s)):
                if self.x_copies is not None:
                    self.x_copies[dz].wait_recv()
                (self.up, self.down)[way].wait_recv()
                if s == 1:
                    add_up(self.span(dz, way, 1), self.own(dz, way, 1) + [self.slot(way, 0, way, 1)])
                    if self.x_copies is not None:
                        add_up(self.span(dz, 1 - way, 1), self.own(dz, 1 - way, 1))
                else:
                    add_up(self.span(dz), self.own(dz) + [self.slot(way, s - 1)])
                sent = links.send(self.span(dz), self.slot(way, s), (z_up, z_down)[way])
                if way == 0:
                    self.up = sent
                else:
                    self.down = sent

        def finish(self):
            if self.x_copies is not None:
                self.x_copies[0].wait_recv()
            self.up.wait_recv()
            self.down.wait_recv()

        def last(self, first, size):
            return self.own(0, first, size) + [self.slot(0, 3, first, size), self.slot(1, 3, first, size)]

    def finish_z(f, b, ring):
        ring.finish()
        far = pl.ds(2 * f + b, 1)
        add_up(x_last.at[0, far], ring.last(1, 1))
        copy = links.send(x_last.at[0, far], x_last.at[1, far], x_far)
        add_up(part.at[f, pl.ds(b, 1)], ring.last(0, 1))
        return copy

    def close_z(f, b, copy):
        copy.wait_recv()
        add_up(
            summed.at[pl.ds(b, 1), :, pl.ds(f * HALF, HALF)],
            [part.at[f, pl.ds(b, 1)], x_last.at[1, pl.ds(2 * f + b, 1)]],
        )

    def close_x(f, ring):
        ring.finish()
        add_up(summed.at[pl.ds(2, 2), :, pl.ds(f * HALF, HALF)], ring.last(0, 2))

    def middle(pair):
        def body(i):
            b = 2 * pair + i
            rows = summed[b]
            pre = jnp.dot(rows, weight[...], preferred_element_type=F32)
            sig = jax.nn.sigmoid(pre)
            hidden[b] = (pre * sig).astype(BF16)
            grad_pre = (cot[b].astype(F32) * sig * (1.0 + pre * (1.0 - sig))).astype(BF16)
            own = lax.dot_general(
                grad_pre, weight[...], (((1,), (1,)), ((), ())), preferred_element_type=F32
            )
            grads[0][b] = own[:, :HALF].astype(BF16)
            grads[1][2 * b] = own[:, HALF:].astype(BF16)
            w_sum[...] += jnp.dot(rows.T, grad_pre, preferred_element_type=F32)

        each(2, body)

    first = gather_first(0)
    for load in (loads[0], loads[1], loads[7]):
        load.wait()
    fill_table(here, count[0, 0], rows_in[...], cols_in[...], lines)
    table_copy = pltpu.make_async_copy(lines, table, local_sem.at[8])
    table_copy.start()
    for load in loads[2:7]:
        load.wait()
    second = gather_y(0, first) + gather_x(0, first)
    first1 = gather_first(1)
    table_copy.wait()
    for f in range(2):
        slots[f, T] = jnp.zeros((T, HALF), BF16)
    w_sum[...] = jnp.zeros_like(w_sum)
    carry[...] = jnp.zeros_like(carry)
    for copy in second:
        copy.wait_recv()
    products(0, 0, 1, False)
    core0 = core_send(0)
    second1 = gather_y(1, first1)
    for over in first1[1]:
        second1 += over.values()
    x0, x1, last = {}, {}, {}
    z0 = [Ring(0, 0), Ring(0, 1)]
    z1 = [Ring(1, 0), Ring(1, 1)]
    ring_x0, ring_x1 = Ring(0, 2, x0), Ring(1, 2, x1)

    def step_all(rings, s):
        for ring in rings:
            ring.step(s)

    for dz in URGENT:
        x0[dz] = core_sum(0, dz, core0)
        if dz == 4:
            step_all(z0, 0)
    step_all(z0, 1)
    ring_x0.step(0)
    for copy in second1:
        copy.wait_recv()
    products(1, 0, 2, False)
    step_all(z0, 2)
    products(1, 1, 2, False)
    core1 = core_send(1)
    step_all(z0, 3)
    ring_x0.step(1)
    for dz in URGENT:
        x1[dz] = core_sum(1, dz, core1)
        if dz == 4:
            step_all(z1, 0)
    ring_x0.step(2)
    step_all(z1, 1)
    ring_x1.step(0)
    for b in range(2):
        last[0, b] = finish_z(0, b, z0[b])
    ring_x0.step(3)
    step_all(z1, 2)
    ring_x1.step(1)
    for b in range(2):
        close_z(0, b, last[0, b])
    step_all(z1, 3)
    ring_x1.step(2)
    close_x(0, ring_x0)
    for b in range(2):
        last[1, b] = finish_z(1, b, z1[b])
    ring_x1.step(3)
    for b in range(2):
        close_z(1, b, last[1, b])
    middle(0)

    class Spread:
        def __init__(self, f, place):
            self.f, self.place = f, place
            self.up = self.down = None

        def span(self, dz, first=0, size=2):
            return grads[self.f].at[pl.ds((dz % 8) * 8 + self.place + first, size)]

        def step(self, s):
            if s > 0:
                self.done()
            first, size = ((0, 2), (1, 1))[s == 3]
            self.up = links.send(self.span(-s, 0, size), self.span(-s - 1, 0, size), z_up)
            self.down = links.send(self.span(s, first, size), self.span(s + 1, first, size), z_down)

        def done(self):
            self.up.wait_recv()
            self.down.wait_recv()

    from_twin = {0: [], 1: []}
    from_far = {}

    def to_twin(f, dz, place, size):
        at = dz * 8 + place
        from_twin[f].append(links.send(grads[f].at[pl.ds(at, size)], grads[f].at[pl.ds(64 + at, size)], twin))

    def to_far(dz, place):
        at = dz * 8 + place
        from_far[dz, place] = links.send(grads[0].at[pl.ds(at, 2)], grads[0].at[pl.ds(at + 4, 2)], x_far)

    def near(b):
        return links.send(grads[1].at[pl.ds(2 * b, 1)], grads[1].at[pl.ds(2 * b + 1, 1)], x_far)

    def around(s):
        return sorted({-s % 8, s % 8})

    late = [Spread(0, 0), Spread(0, 2)]
    early = [Spread(1, 2 * b) for b in range(4)]

    def late_round(s):
        for stream in late:
            if s < 4:
                stream.step(s)
            else:
                stream.done()
            for dz in around(s):
                to_far(dz, stream.place)
        for dz in around(s):
            to_twin(0, dz, 0, 4)

    def early_round(s):
        for b, stream in enumerate(early):
            if s == 0:
                nears[b].wait_recv()
            if s < 4:
                stream.step(s)
            else:
                stream.done()
            if b % 2:
                for dz in around(s):
                    to_twin(1, dz, 4 * (b // 2), 4)

    def far_to_twin(s):
        for dz in around(s):
            for place in (0, 2):
                from_far[dz, place].wait_recv()
            to_twin(0, dz, 4, 4)

    def all_here(f):
        for copy in from_twin[f]:
            copy.wait_recv()

    nears = [near(0), near(1)]
    late[0].step(0)
    to_far(0, 0)
    close_x(1, ring_x1)
    middle(1)
    nears += [near(2), near(3)]
    late[1].step(0)
    to_far(0, 2)
    to_twin(0, 0, 0, 4)

    def weight_start():
        def fill(i):
            for j in range(2):
                w_own[2 * i + j] = w_sum[pl.ds(8 * i, 8), j * 128 : (j + 1) * 128]

        each(32, fill)
        return links.send(w_own.at[pl.ds((1 - here["core"]) * 32, 32)], w_core.at[0], twin)

    def weight_y(copy):
        copy.wait_recv()

        def fill(i):
            w_core[1, i] = w_own[here["core"] * 32 + i] + w_core[0, i]

        each(32, fill)
        return [
            links.send(w_core.at[1, pl.ds(lax.rem(here["y"] + d, 4) * 8, 8)], w_y.at[d], y_to[d]) for d in (1, 2, 3)
        ]

    def weight_z(copies):
        for copy in copies:
            copy.wait_recv()

        def fill(i):
            w_y[0, i] = w_core[1, here["y"] * 8 + i] + w_y[1, i] + w_y[2, i] + w_y[3, i]

        each(8, fill)
        return [
            links.send(w_y.at[0, pl.ds(lax.rem(here["z"] + d, 8), 1)], w_z.at[pl.ds(d, 1)], z_to[d])
            for d in range(1, 8)
        ]

    def weight_x(copies):
        for copy in copies:
            copy.wait_recv()
        total = w_y[0, pl.ds(here["z"], 1)]
        for d in range(1, 8):
            total = total + w_z[d : d + 1]
        w_x[0:1] = total
        return [
            links.send(w_x.at[pl.ds(0, 1)], w_x.at[pl.ds(i, 1)], to)
            for i, to in ((1, x_far), (2, x_near), (3, x_both))
        ]

    def weight_all_z(copies):
        for copy in copies:
            copy.wait_recv()
        mine = pl.ds(here["z"], 1)
        w_all_z[mine] = (w_x[0:1] + w_x[1:2]) + (w_x[2:3] + w_x[3:4])
        return [links.send(w_all_z.at[mine], w_all_z.at[mine], z_to[d]) for d in range(1, 8)]

    def weight_all_y(copies):
        for copy in copies:
            copy.wait_recv()
        mine = pl.ds(here["y"] * 8, 8)

        def fill(i):
            w_all_y[here["y"] * 8 + i] = w_all_z[i]

        each(8, fill)
        return [links.send(w_all_y.at[mine], w_all_y.at[mine], y_to[d]) for d in (1, 2, 3)]

    def weight_all_core(copies):
        for copy in copies:
            copy.wait_recv()
        mine = pl.ds(here["core"] * 32, 32)

        def fill(i):
            w_all[here["core"] * 32 + i] = w_all_y[i]

        each(32, fill)
        return links.send(w_all.at[mine], w_all.at[mine], twin)

    def weight_end(copy):
        copy.wait_recv()

        def fill(i):
            for j in range(2):
                grad_weight[pl.ds(8 * i, 8), j * 128 : (j + 1) * 128] = w_all[2 * i + j]

        each(32, fill)

    def back_first(f):
        def fill(place):
            back[f, place] = slots[f, table[COL_LAST, place]]

        each(32, fill)
        near_copies = {
            d: links.send(back.at[f, pl.ds((4 + d) * 4, 2)], back_x.at[f, pl.ds(d * 2, 2)], x_near)
            for d in (2, 1, 3, 0)
        }
        y_copies = [
            links.send(back.at[f, pl.ds((x_other * 4 + d) * 4 + 2, 2)], back_y.at[f, d, pl.ds(x_other * 2, 2)], y_to[d])
            for x_other in (1, 0)
            for d in (2, 1, 3)
        ]
        return near_copies, y_copies

    def back_second(f, first):
        near_copies, y_copies = first
        y_second = []
        for d in (2, 1, 3, 0):
            near_copies[d].wait_recv()
            own = back.at[f, pl.ds(d * 4, 2)]
            add_up(own, [own, back_x.at[f, pl.ds(d * 2, 2)]])
            if d:
                y_second.append(links.send(back.at[f, pl.ds(d * 4, 2)], back_y2.at[f, d], y_to[d]))
        for copy in y_copies[:3]:
            copy.wait_recv()
        add_up(
            back_x2.at[f, pl.ds(0, 2)],
            [back.at[f, pl.ds(18, 2)]] + [back_y.at[f, d, pl.ds(2, 2)] for d in (1, 2, 3)],
        )
        near_second = links.send(back_x2.at[f, pl.ds(0, 2)], back_x2.at[f, pl.ds(2, 2)], x_near)
        return y_copies[3:], y_second, near_second

    def back_third(f, second):
        y_copies, y_second, near_second = second
        lanes = pl.ds(f * HALF, HALF)
        for copy in y_copies + [near_second]:
            copy.wait_recv()
        add_up(
            grad_feat.at[pl.ds(2, 2), :, lanes],
            [back.at[f, pl.ds(2, 2)], back_x2.at[f, pl.ds(2, 2)]]
            + [back_y.at[f, d, pl.ds(0, 2)] for d in (1, 2, 3)],
        )
        for copy in y_second:
            copy.wait_recv()
        add_up(
            grad_feat.at[pl.ds(0, 2), :, lanes],
            [back.at[f, pl.ds(0, 2)]] + [back_y2.at[f, d] for d in (1, 2, 3)],
        )

    w_copy = weight_start()
    late_round(1)
    early_round(0)
    w_copy = weight_y(w_copy)
    late_round(2)
    early_round(1)
    late_round(3)
    w_copy = weight_z(w_copy)
    far_to_twin(0)
    far_to_twin(1)
    early_round(2)
    late_round(4)
    w_copy = weight_x(w_copy)
    far_to_twin(2)
    early_round(3)
    w_copy = weight_all_z(w_copy)
    far_to_twin(3)
    far_to_twin(4)
    all_here(0)
    products(0, 0, 1, True)
    first0 = back_first(0)
    early_round(4)
    w_copy = weight_all_y(w_copy)
    all_here(1)
    products(1, 0, 2, True)
    second0 = back_second(0, first0)
    products(1, 1, 2, True)
    first1 = back_first(1)
    w_copy = weight_all_core(w_copy)
    back_third(0, second0)
    second1 = back_second(1, first1)
    weight_end(w_copy)
    back_third(1, second1)
    for copy in links.copies:
        copy.wait_send()


def finish_kernel(*refs):
    copies = [pltpu.make_async_copy(refs[i], refs[3 + i], refs[6].at[i]) for i in range(3)]
    for copy in copies:
        copy.start()
    for copy in copies:
        copy.wait()


def per_device(features, weight, cotangent, tile_rows, tile_cols, tile_values, tile_count):
    hbm, vmem = pl.BlockSpec(memory_space=pl.ANY), pl.BlockSpec(memory_space=pltpu.VMEM)

    def blocks(*counts):
        return pltpu.VMEM((*counts, T, HALF), BF16)

    def pieces(*counts):
        return pltpu.VMEM((*counts, 8, 128), F32)

    out_shape = (
        jax.ShapeDtypeStruct((4, T, 256), BF16),
        jax.ShapeDtypeStruct((4, T, 256), BF16),
        jax.ShapeDtypeStruct((256, 256), F32),
    )
    hidden, grad_feat, grad_weight = pl.pallas_call(
        layer_kernel,
        out_shape=out_shape,
        in_specs=[hbm] * 7,
        out_specs=(vmem, vmem, vmem),
        scratch_shapes=[
            pltpu.SMEM((LINES, T), jnp.int32),
            pltpu.VMEM((LINES, T), jnp.int32),
            pltpu.SMEM((1, 1), jnp.int32),
            pltpu.VMEM((1, T), jnp.int32),
            pltpu.VMEM((1, T), jnp.int32),
            pltpu.VMEM((256, 256), BF16),
            blocks(T),
            pltpu.VMEM((4, T, 256), BF16),
            blocks(32),
            blocks(32),
            blocks(2, T + 1),
            blocks(2, 64),
            blocks(2, 64),
            blocks(2, 64),
            blocks(2, 16),
            blocks(2, 3, 2, 8),
            blocks(2, 4),
            pltpu.VMEM((2, 2, T, HALF), F32),
            pltpu.VMEM((4, T, 256), BF16),
            blocks(128),
            blocks(128),
            pltpu.VMEM((T, HALF), F32),
            blocks(2, 32),
            blocks(2, 8),
            blocks(2, 4, 4),
            blocks(2, 4, 2),
            blocks(2, 4),
            pltpu.VMEM((256, 256), F32),
            pieces(64),
            pieces(2, 32),
            pieces(4, 8),
            pieces(8),
            pieces(4),
            pieces(8),
            pieces(32),
            pieces(64),
            pltpu.SemaphoreType.DMA((9,)),
            pltpu.SemaphoreType.DMA((COPIES,)),
            pltpu.SemaphoreType.DMA((COPIES,)),
        ],
        compiler_params=pltpu.CompilerParams(
            collective_id=0, has_side_effects=True, vmem_limit_bytes=60 * 2**20
        ),
        cost_estimate=pl.CostEstimate(flops=5 * 10**9, bytes_accessed=6 * 2**20, transcendentals=2**17),
        name="layer",
    )(
        tile_count,
        tile_rows.reshape(1, T),
        tile_cols.reshape(1, T),
        features.reshape(4, T, 256),
        weight,
        cotangent.reshape(4, T, 256),
        tile_values.reshape(T, T, T),
    )
    hidden, grad_feat, grad_weight = pl.pallas_call(
        finish_kernel,
        out_shape=out_shape,
        in_specs=[hbm] * 3,
        out_specs=[vmem] * 3,
        scratch_shapes=[pltpu.SemaphoreType.DMA((3,))],
        name="finish",
    )(hidden, grad_feat, grad_weight)
    return hidden.reshape(4 * T, 256), grad_feat.reshape(4 * T, 256), grad_weight


def solution(mesh):
    placed = (
        P(("row", "col"), None),
        P(),
        P(("row", "col"), None),
        P("row", "col", None),
        P("row", "col", None),
        P("row", "col", None, None, None),
        P("row", "col"),
    )
    return jax.shard_map(
        per_device,
        mesh=mesh,
        in_specs=placed,
        out_specs=(P(("row", "col"), None), P(("row", "col"), None), P()),
        check_vma=False,
    )
```

```python
import functools

import jax
import jax.numpy as jnp
from jax import lax
from jax.experimental import pallas as pl
from jax.experimental.pallas import tpu as pltpu
from jax.sharding import PartitionSpec as P

MESH = pl.DeviceIdType.MESH
BF16 = jnp.bfloat16
F32 = jnp.float32
T = 128
HALF = 128
COPIES = 340
GROUP = 64
URGENT = (4, 3, 5, 2, 6, 1, 7, 0)


def position():
    row, col = lax.axis_index("row"), lax.axis_index("col")
    return dict(
        x_hi=col // 16, z=lax.rem(col // 2, 8), core=lax.rem(col, 2), y=row // 2, x_lo=lax.rem(row, 2)
    )


def device(here, x_hi=0, x_lo=0, y=0, z=0, core=0):
    x_hi = 1 - here["x_hi"] if x_hi else here["x_hi"]
    x_lo = 1 - here["x_lo"] if x_lo else here["x_lo"]
    core = 1 - here["core"] if core else here["core"]
    y = lax.rem(here["y"] + y, 4)
    z = lax.rem(here["z"] + z, 8)
    return (y * 2 + x_lo, x_hi * 16 + z * 2 + core)


ROW_TILE, ROW_KEEP, ROW_LAST, ROW_FEAT, COL_TILE, COL_KEEP, COL_LAST, COL_GRAD = range(8)
LINES = 16


def fill_table(here, count, rows, cols, table_ref):
    lane = lax.broadcasted_iota(jnp.int32, (T, T), 1)
    sub = lax.broadcasted_iota(jnp.int32, (T, T), 0)
    eye = lane == sub

    def spread(values):
        return jnp.broadcast_to(values, (T, T))

    def column(values):
        return jnp.broadcast_to(jnp.sum(jnp.where(eye, spread(values), 0), axis=1, keepdims=True), (T, T))

    def total(values):
        return jnp.sum(values, axis=0, keepdims=True)

    live_down = sub < count

    def feat_place(cols):
        owner = cols // 4
        return ((lax.rem(owner, 2) + here["x_lo"]) % 2 * 4 + (owner // 2 - here["y"] + 4) % 4) * 4 + lax.rem(cols, 4)

    def row_place(rows, order):
        owner, block = rows // 4, lax.rem(rows, 4)
        x_other = (owner // 16 + here["x_hi"]) % 2
        z_away = (lax.rem(owner // 2, 8) - here["z"] + 8) % 8
        core_other = (lax.rem(owner, 2) + here["core"]) % 2
        return (core_other * 8 + z_away) * 8 + order(block, x_other)

    def sum_order(block, x_other):
        return jnp.where(block < 2, 2 * block + x_other, 2 + block + 2 * x_other)

    def far_last(block, x_other):
        return block + 4 * x_other

    def far_first(block, x_other):
        return 2 * block + x_other

    rows_down, cols_down = column(rows), feat_place(column(cols))
    grads_down = [row_place(rows_down, far_last), row_place(rows_down, far_first)]
    rows_down = row_place(rows_down, sum_order)
    rows, cols = row_place(rows, sum_order), feat_place(cols)

    def sorted_by(keys, keys_down, values_down):
        big = T * T
        key = jnp.where(lane < count, spread(keys) * T + lane, big + lane)
        key_down = jnp.where(live_down, keys_down * T + sub, big + sub)
        rank_down = jnp.sum(jnp.where(key < key_down, 1, 0), axis=1, keepdims=True)
        rank_down = jnp.broadcast_to(rank_down, (T, T))
        now = rank_down == lane
        tile = total(jnp.where(now, sub, 0))
        values = [total(jnp.where(now, value, 0)) for value in values_down]
        mine = total(jnp.where(now, keys_down, 0))
        before = total(jnp.where(rank_down == lane - 1, keys_down, 0))
        first = lax.broadcasted_iota(jnp.int32, (1, T), 1) == 0
        keep = jnp.where(jnp.logical_or(first, mine != before), 0, 1)
        upto = total(jnp.where(jnp.logical_and(live_down, keys_down <= lane), 1, 0))
        some = total(jnp.where(jnp.logical_and(live_down, keys_down == lane), 1, 0))
        return [tile, keep, jnp.where(some > 0, upto - 1, T), *values]

    lines = sorted_by(rows, rows_down, [cols_down]) + sorted_by(cols, cols_down, grads_down)
    table_ref[...] = jnp.zeros_like(table_ref)
    for number, line in enumerate(lines):
        table_ref[number : number + 1, :] = line


def each(count, body):
    def step(i, carried):
        body(i)
        return carried

    lax.fori_loop(0, count, step, 0)


def add_up(out, terms):
    def body(i):
        rows = pl.ds(i * 32, 32)
        total = terms[0][:, rows].astype(F32)
        for term in terms[1:]:
            total = total + term[:, rows].astype(F32)
        out[:, rows] = total.astype(out.dtype)

    each(T // 32, body)


class Links:
    def __init__(self, send_sem, recv_sem):
        self.send_sem, self.recv_sem, self.copies = send_sem, recv_sem, []

    def send(self, src, dst, to):
        number = len(self.copies)
        copy = pltpu.make_async_remote_copy(
            src_ref=src,
            dst_ref=dst,
            send_sem=self.send_sem.at[number],
            recv_sem=self.recv_sem.at[number],
            device_id=to,
            device_id_type=MESH,
        )
        copy.start()
        self.copies.append(copy)
        return copy


def layer_kernel(
    count_hbm,
    rows_hbm,
    cols_hbm,
    feat_hbm,
    weight_hbm,
    cot_hbm,
    tile_hbm,
    hidden,
    grad_feat,
    grad_weight,
    table,
    lines,
    count,
    rows_in,
    cols_in,
    weight,
    tiles,
    cot,
    feats0,
    feats1,
    slots,
    give,
    core_in,
    value,
    x_in,
    ring_in,
    x_last,
    part,
    summed,
    grads0,
    grads1,
    carry,
    back,
    back_x,
    back_y,
    back_y2,
    back_x2,
    w_sum,
    w_own,
    w_core,
    w_y,
    w_z,
    w_x,
    w_all_z,
    w_all_y,
    w_all,
    local_sem,
    send_sem,
    recv_sem,
):
    here = position()
    feats, grads = (feats0, feats1), (grads0, grads1)
    links = Links(send_sem, recv_sem)
    z_up, z_down = device(here, z=1), device(here, z=7)
    x_far, x_near = device(here, x_hi=1), device(here, x_lo=1)
    x_both = device(here, x_hi=1, x_lo=1)
    twin = device(here, core=1)
    y_to = {d: device(here, y=d) for d in (1, 2, 3)}
    z_to = {d: device(here, z=d) for d in range(1, 8)}

    feat_own = [feat_hbm.at[:, :, pl.ds(f * HALF, HALF)] for f in range(2)]
    moves = [
        (rows_hbm, rows_in),
        (cols_hbm, cols_in),
        (feat_own[0], feats[0].at[pl.ds(0, 4)]),
        (feat_own[1], feats[1].at[pl.ds(0, 4)]),
        (tile_hbm, tiles),
        (weight_hbm, weight),
        (cot_hbm, cot),
        (count_hbm, count),
    ]
    loads = [pltpu.make_async_copy(src, dst, local_sem.at[i]) for i, (src, dst) in enumerate(moves)]
    for load in loads:
        load.start()

    barrier = pltpu.get_barrier_semaphore()
    partners = [x_far, x_near, twin, z_up, z_down, *y_to.values()]
    for partner in partners:
        pl.semaphore_signal(barrier, inc=1, device_id=partner, device_id_type=MESH)
    pl.semaphore_wait(barrier, len(partners))

    def over(f, src, place, size=2):
        return {d: links.send(src, feats[f].at[pl.ds((4 - d) * 4 + place, size)], y_to[d]) for d in (1, 3)}

    def relay(f, copies, place, size=1):
        sent = []
        for d, group, first in ((1, 12, 0), (3, 4, size)):
            copies[d].wait_recv()
            src = feats[f].at[pl.ds(group + place + first, size)]
            sent.append(links.send(src, feats[f].at[pl.ds(8 + place + first, size)], y_to[d]))
        return sent

    def across(f, group):
        rows = group * 4 + 2
        return links.send(feats[f].at[pl.ds(rows, 2)], feats[f].at[pl.ds(16 + rows, 2)], x_near)

    def gather_mixed():
        own = [feat_own[0].at[pl.ds(b, 2)] for b in (0, 2)]
        near = [links.send(own[0], feats[0].at[pl.ds(16, 2)], x_near)]
        late = over(0, own[1], 2)
        near.append(links.send(own[1], feats[0].at[pl.ds(18, 2)], x_near))
        return near, late, over(0, own[0], 0)

    def gather_rest(first):
        near, late, early = first
        late_two = relay(0, late, 2)
        copies = [near[1], across(0, 3), across(0, 1)]
        near[0].wait_recv()
        near_over = over(0, feats[0].at[pl.ds(16, 2)], 16)
        copies += relay(0, early, 0)
        for copy in late_two:
            copy.wait_recv()
        copies.append(across(0, 2))
        return copies + relay(0, near_over, 16)

    def gather_plain():
        own = feat_own[1]
        copies = [links.send(own, feats[1].at[pl.ds((4 - d) * 4, 4)], y_to[d]) for d in (2, 1, 3)]
        return links.send(own, feats[1].at[pl.ds(16, 4)], x_near), copies

    def gather_near(first):
        near, copies = first
        near.wait_recv()
        return copies + [
            links.send(feats[1].at[pl.ds(16, 4)], feats[1].at[pl.ds(16 + (4 - d) * 4, 4)], y_to[d])
            for d in (2, 1, 3)
        ]

    def products(f, piece, pieces, back_pass):
        tile_line, value_line, keep_line = (
            (COL_TILE, COL_GRAD + f, COL_KEEP) if back_pass else (ROW_TILE, ROW_FEAT, ROW_KEEP)
        )
        steps = T // GROUP // pieces
        source = (grads if back_pass else feats)[f]

        def step(i):
            total = carry[...]
            for u in range(GROUP):
                t = i * GROUP + u
                tile = tiles[table[tile_line, t]]
                block = source[table[value_line, t]]
                if back_pass:
                    tile = tile.T
                term = jnp.dot(tile, block, preferred_element_type=F32)
                total = term + total * table[keep_line, t].astype(F32)
                slots[f, t] = total.astype(BF16)
            carry[...] = total

        each(steps, lambda i: step(piece * steps + i))

    def core_send(f):
        copies = {}
        for dz in URGENT:

            def fill(place, dz=dz):
                give[f, dz * 8 + place] = slots[f, table[ROW_LAST, 64 + dz * 8 + place]]

            each(8, fill)
            span = pl.ds(dz * 8, 8)
            copies[dz] = links.send(give.at[f, span], core_in.at[f, span], twin)
        return copies

    def core_sum(f, dz, copies):
        copies[dz].wait_recv()

        def fill(place):
            at = dz * 8 + place
            own = slots[f, table[ROW_LAST, at]].astype(F32)
            value[f, at] = (own + core_in[f, at].astype(F32)).astype(BF16)

        each(8, fill)
        return links.send(value.at[f, pl.ds(dz * 8 + 6, 2)], x_in.at[f, pl.ds(dz * 2, 2)], x_far)

    class Ring:
        def __init__(self, f, stream, x_copies=None):
            self.f, self.stream, self.x_copies = f, stream, x_copies
            self.up = self.down = None

        def span(self, dz, first=0, size=2):
            return value.at[self.f, pl.ds(dz * 8 + self.stream * 2 + first, size)]

        def own(self, dz, first=0, size=2):
            if self.x_copies is None:
                return [self.span(dz, first, size)]
            return [self.span(dz, first, size), x_in.at[self.f, pl.ds(dz * 2 + first, size)]]

        def slot(self, way, step, first=0, size=2):
            return ring_in.at[self.f, self.stream, way, pl.ds(step * 2 + first, size)]

        def step(self, s):
            if s == 0:
                if self.x_copies is not None:
                    self.x_copies[4].wait_recv()
                    add_up(self.span(4), self.own(4))
                self.up = links.send(self.span(4, 0, 1), self.slot(0, 0, 0, 1), z_up)
                self.down = links.send(self.span(4, 1, 1), self.slot(1, 0, 1, 1), z_down)
                return
            for way, dz in ((0, 4 - s), (1, 4 + s)):
                if self.x_copies is not None:
                    self.x_copies[dz].wait_recv()
                (self.up, self.down)[way].wait_recv()
                if s == 1:
                    add_up(self.span(dz, way, 1), self.own(dz, way, 1) + [self.slot(way, 0, way, 1)])
                    if self.x_copies is not None:
                        add_up(self.span(dz, 1 - way, 1), self.own(dz, 1 - way, 1))
                else:
                    add_up(self.span(dz), self.own(dz) + [self.slot(way, s - 1)])
                sent = links.send(self.span(dz), self.slot(way, s), (z_up, z_down)[way])
                if way == 0:
                    self.up = sent
                else:
                    self.down = sent

        def finish(self):
            if self.x_copies is not None:
                self.x_copies[0].wait_recv()
            self.up.wait_recv()
            self.down.wait_recv()

        def last(self, first, size):
            return self.own(0, first, size) + [self.slot(0, 3, first, size), self.slot(1, 3, first, size)]

    def finish_z(f, b, ring):
        ring.finish()
        far = pl.ds(2 * f + b, 1)
        add_up(x_last.at[0, far], ring.last(1, 1))
        copy = links.send(x_last.at[0, far], x_last.at[1, far], x_far)
        add_up(part.at[f, pl.ds(b, 1)], ring.last(0, 1))
        return copy

    def close_z(f, b, copy):
        copy.wait_recv()
        add_up(
            summed.at[pl.ds(b, 1), :, pl.ds(f * HALF, HALF)],
            [part.at[f, pl.ds(b, 1)], x_last.at[1, pl.ds(2 * f + b, 1)]],
        )

    def close_x(f, ring):
        ring.finish()
        add_up(summed.at[pl.ds(2, 2), :, pl.ds(f * HALF, HALF)], ring.last(0, 2))

    def middle(pair):
        def body(i):
            b = 2 * pair + i
            rows = summed[b]
            pre = jnp.dot(rows, weight[...], preferred_element_type=F32)
            sig = jax.nn.sigmoid(pre)
            hidden[b] = (pre * sig).astype(BF16)
            grad_pre = (cot[b].astype(F32) * sig * (1.0 + pre * (1.0 - sig))).astype(BF16)
            own = lax.dot_general(
                grad_pre, weight[...], (((1,), (1,)), ((), ())), preferred_element_type=F32
            )
            grads[0][b] = own[:, :HALF].astype(BF16)
            grads[1][2 * b] = own[:, HALF:].astype(BF16)
            w_sum[...] += jnp.dot(rows.T, grad_pre, preferred_element_type=F32)

        each(2, body)

    first = gather_mixed()
    for load in (loads[0], loads[1], loads[7]):
        load.wait()
    fill_table(here, count[0, 0], rows_in[...], cols_in[...], lines)
    table_copy = pltpu.make_async_copy(lines, table, local_sem.at[8])
    table_copy.start()
    for load in loads[2:7]:
        load.wait()
    second = gather_rest(first)
    first1 = gather_plain()
    table_copy.wait()
    for f in range(2):
        slots[f, T] = jnp.zeros((T, HALF), BF16)
    w_sum[...] = jnp.zeros_like(w_sum)
    carry[...] = jnp.zeros_like(carry)
    for copy in second:
        copy.wait_recv()
    products(0, 0, 1, False)
    core0 = core_send(0)
    second1 = gather_near(first1)
    x0, x1, last = {}, {}, {}
    z0 = [Ring(0, 0), Ring(0, 1)]
    z1 = [Ring(1, 0), Ring(1, 1)]
    ring_x0, ring_x1 = Ring(0, 2, x0), Ring(1, 2, x1)

    def step_all(rings, s):
        for ring in rings:
            ring.step(s)

    for dz in URGENT:
        x0[dz] = core_sum(0, dz, core0)
        if dz == 4:
            step_all(z0, 0)
    step_all(z0, 1)
    ring_x0.step(0)
    for copy in second1:
        copy.wait_recv()
    products(1, 0, 2, False)
    step_all(z0, 2)
    products(1, 1, 2, False)
    core1 = core_send(1)
    step_all(z0, 3)
    ring_x0.step(1)
    for dz in URGENT:
        x1[dz] = core_sum(1, dz, core1)
        if dz == 4:
            step_all(z1, 0)
    ring_x0.step(2)
    step_all(z1, 1)
    ring_x1.step(0)
    for b in range(2):
        last[0, b] = finish_z(0, b, z0[b])
    ring_x0.step(3)
    step_all(z1, 2)
    ring_x1.step(1)
    for b in range(2):
        close_z(0, b, last[0, b])
    step_all(z1, 3)
    ring_x1.step(2)
    close_x(0, ring_x0)
    for b in range(2):
        last[1, b] = finish_z(1, b, z1[b])
    ring_x1.step(3)
    for b in range(2):
        close_z(1, b, last[1, b])
    middle(0)

    class Spread:
        def __init__(self, f, place):
            self.f, self.place = f, place
            self.up = self.down = None

        def span(self, dz, first=0, size=2):
            return grads[self.f].at[pl.ds((dz % 8) * 8 + self.place + first, size)]

        def step(self, s):
            if s > 0:
                self.done()
            first, size = ((0, 2), (1, 1))[s == 3]
            self.up = links.send(self.span(-s, 0, size), self.span(-s - 1, 0, size), z_up)
            self.down = links.send(self.span(s, first, size), self.span(s + 1, first, size), z_down)

        def done(self):
            self.up.wait_recv()
            self.down.wait_recv()

    from_twin = {0: [], 1: []}
    from_far = {}

    def to_twin(f, dz, place, size):
        at = dz * 8 + place
        from_twin[f].append(links.send(grads[f].at[pl.ds(at, size)], grads[f].at[pl.ds(64 + at, size)], twin))

    def to_far(dz, place):
        at = dz * 8 + place
        from_far[dz, place] = links.send(grads[0].at[pl.ds(at, 2)], grads[0].at[pl.ds(at + 4, 2)], x_far)

    def near(b):
        return links.send(grads[1].at[pl.ds(2 * b, 1)], grads[1].at[pl.ds(2 * b + 1, 1)], x_far)

    def around(s):
        return sorted({-s % 8, s % 8})

    late = [Spread(0, 0), Spread(0, 2)]
    early = [Spread(1, 2 * b) for b in range(4)]

    def late_round(s):
        for stream in late:
            if s < 4:
                stream.step(s)
            else:
                stream.done()
            for dz in around(s):
                to_far(dz, stream.place)
        for dz in around(s):
            to_twin(0, dz, 0, 4)

    def early_round(s):
        for b, stream in enumerate(early):
            if s == 0:
                nears[b].wait_recv()
            if s < 4:
                stream.step(s)
            else:
                stream.done()
            if b % 2:
                for dz in around(s):
                    to_twin(1, dz, 4 * (b // 2), 4)

    def far_to_twin(s):
        for dz in around(s):
            for place in (0, 2):
                from_far[dz, place].wait_recv()
            to_twin(0, dz, 4, 4)

    def all_here(f):
        for copy in from_twin[f]:
            copy.wait_recv()

    nears = [near(0), near(1)]
    late[0].step(0)
    to_far(0, 0)
    close_x(1, ring_x1)
    middle(1)
    nears += [near(2), near(3)]
    late[1].step(0)
    to_far(0, 2)
    to_twin(0, 0, 0, 4)

    def weight_start():
        def fill(i):
            for j in range(2):
                w_own[2 * i + j] = w_sum[pl.ds(8 * i, 8), j * 128 : (j + 1) * 128]

        each(32, fill)
        return links.send(w_own.at[pl.ds((1 - here["core"]) * 32, 32)], w_core.at[0], twin)

    def weight_y(copy):
        copy.wait_recv()

        def fill(i):
            w_core[1, i] = w_own[here["core"] * 32 + i] + w_core[0, i]

        each(32, fill)
        return [
            links.send(w_core.at[1, pl.ds(lax.rem(here["y"] + d, 4) * 8, 8)], w_y.at[d], y_to[d]) for d in (1, 2, 3)
        ]

    def weight_z(copies):
        for copy in copies:
            copy.wait_recv()

        def fill(i):
            w_y[0, i] = w_core[1, here["y"] * 8 + i] + w_y[1, i] + w_y[2, i] + w_y[3, i]

        each(8, fill)
        return [
            links.send(w_y.at[0, pl.ds(lax.rem(here["z"] + d, 8), 1)], w_z.at[pl.ds(d, 1)], z_to[d])
            for d in range(1, 8)
        ]

    def weight_x(copies):
        for copy in copies:
            copy.wait_recv()
        total = w_y[0, pl.ds(here["z"], 1)]
        for d in range(1, 8):
            total = total + w_z[d : d + 1]
        w_x[0:1] = total
        return [
            links.send(w_x.at[pl.ds(0, 1)], w_x.at[pl.ds(i, 1)], to)
            for i, to in ((1, x_far), (2, x_near), (3, x_both))
        ]

    def weight_all_z(copies):
        for copy in copies:
            copy.wait_recv()
        mine = pl.ds(here["z"], 1)
        w_all_z[mine] = (w_x[0:1] + w_x[1:2]) + (w_x[2:3] + w_x[3:4])
        return [links.send(w_all_z.at[mine], w_all_z.at[mine], z_to[d]) for d in range(1, 8)]

    def weight_all_y(copies):
        for copy in copies:
            copy.wait_recv()
        mine = pl.ds(here["y"] * 8, 8)

        def fill(i):
            w_all_y[here["y"] * 8 + i] = w_all_z[i]

        each(8, fill)
        return [links.send(w_all_y.at[mine], w_all_y.at[mine], y_to[d]) for d in (1, 2, 3)]

    def weight_all_core(copies):
        for copy in copies:
            copy.wait_recv()
        mine = pl.ds(here["core"] * 32, 32)

        def fill(i):
            w_all[here["core"] * 32 + i] = w_all_y[i]

        each(32, fill)
        return links.send(w_all.at[mine], w_all.at[mine], twin)

    def weight_end(copy):
        copy.wait_recv()

        def fill(i):
            for j in range(2):
                grad_weight[pl.ds(8 * i, 8), j * 128 : (j + 1) * 128] = w_all[2 * i + j]

        each(32, fill)

    def back_first(f):
        def fill(place):
            back[f, place] = slots[f, table[COL_LAST, place]]

        each(32, fill)
        near_copies = {
            d: links.send(back.at[f, pl.ds((4 + d) * 4, 2)], back_x.at[f, pl.ds(d * 2, 2)], x_near)
            for d in (2, 1, 3, 0)
        }
        y_copies = [
            links.send(back.at[f, pl.ds((x_other * 4 + d) * 4 + 2, 2)], back_y.at[f, d, pl.ds(x_other * 2, 2)], y_to[d])
            for x_other in (1, 0)
            for d in (2, 1, 3)
        ]
        return near_copies, y_copies

    def back_second(f, first):
        near_copies, y_copies = first
        y_second = []
        for d in (2, 1, 3, 0):
            near_copies[d].wait_recv()
            own = back.at[f, pl.ds(d * 4, 2)]
            add_up(own, [own, back_x.at[f, pl.ds(d * 2, 2)]])
            if d:
                y_second.append(links.send(back.at[f, pl.ds(d * 4, 2)], back_y2.at[f, d], y_to[d]))
        for copy in y_copies[:3]:
            copy.wait_recv()
        add_up(
            back_x2.at[f, pl.ds(0, 2)],
            [back.at[f, pl.ds(18, 2)]] + [back_y.at[f, d, pl.ds(2, 2)] for d in (1, 2, 3)],
        )
        near_second = links.send(back_x2.at[f, pl.ds(0, 2)], back_x2.at[f, pl.ds(2, 2)], x_near)
        return y_copies[3:], y_second, near_second

    def back_third(f, second):
        y_copies, y_second, near_second = second
        lanes = pl.ds(f * HALF, HALF)
        for copy in y_copies + [near_second]:
            copy.wait_recv()
        add_up(
            grad_feat.at[pl.ds(2, 2), :, lanes],
            [back.at[f, pl.ds(2, 2)], back_x2.at[f, pl.ds(2, 2)]]
            + [back_y.at[f, d, pl.ds(0, 2)] for d in (1, 2, 3)],
        )
        for copy in y_second:
            copy.wait_recv()
        add_up(
            grad_feat.at[pl.ds(0, 2), :, lanes],
            [back.at[f, pl.ds(0, 2)]] + [back_y2.at[f, d] for d in (1, 2, 3)],
        )

    w_copy = weight_start()
    late_round(1)
    early_round(0)
    w_copy = weight_y(w_copy)
    late_round(2)
    early_round(1)
    late_round(3)
    w_copy = weight_z(w_copy)
    far_to_twin(0)
    far_to_twin(1)
    early_round(2)
    late_round(4)
    w_copy = weight_x(w_copy)
    far_to_twin(2)
    early_round(3)
    w_copy = weight_all_z(w_copy)
    far_to_twin(3)
    far_to_twin(4)
    all_here(0)
    products(0, 0, 1, True)
    first0 = back_first(0)
    early_round(4)
    w_copy = weight_all_y(w_copy)
    all_here(1)
    products(1, 0, 2, True)
    second0 = back_second(0, first0)
    products(1, 1, 2, True)
    first1 = back_first(1)
    w_copy = weight_all_core(w_copy)
    back_third(0, second0)
    second1 = back_second(1, first1)
    weight_end(w_copy)
    back_third(1, second1)
    for copy in links.copies:
        copy.wait_send()


def finish_kernel(*refs):
    copies = [pltpu.make_async_copy(refs[i], refs[3 + i], refs[6].at[i]) for i in range(3)]
    for copy in copies:
        copy.start()
    for copy in copies:
        copy.wait()


def per_device(features, weight, cotangent, tile_rows, tile_cols, tile_values, tile_count):
    hbm, vmem = pl.BlockSpec(memory_space=pl.ANY), pl.BlockSpec(memory_space=pltpu.VMEM)

    def blocks(*counts):
        return pltpu.VMEM((*counts, T, HALF), BF16)

    def pieces(*counts):
        return pltpu.VMEM((*counts, 8, 128), F32)

    out_shape = (
        jax.ShapeDtypeStruct((4, T, 256), BF16),
        jax.ShapeDtypeStruct((4, T, 256), BF16),
        jax.ShapeDtypeStruct((256, 256), F32),
    )
    hidden, grad_feat, grad_weight = pl.pallas_call(
        layer_kernel,
        out_shape=out_shape,
        in_specs=[hbm] * 7,
        out_specs=(vmem, vmem, vmem),
        scratch_shapes=[
            pltpu.SMEM((LINES, T), jnp.int32),
            pltpu.VMEM((LINES, T), jnp.int32),
            pltpu.SMEM((1, 1), jnp.int32),
            pltpu.VMEM((1, T), jnp.int32),
            pltpu.VMEM((1, T), jnp.int32),
            pltpu.VMEM((256, 256), BF16),
            blocks(T),
            pltpu.VMEM((4, T, 256), BF16),
            blocks(32),
            blocks(32),
            blocks(2, T + 1),
            blocks(2, 64),
            blocks(2, 64),
            blocks(2, 64),
            blocks(2, 16),
            blocks(2, 3, 2, 8),
            blocks(2, 4),
            pltpu.VMEM((2, 2, T, HALF), F32),
            pltpu.VMEM((4, T, 256), BF16),
            blocks(128),
            blocks(128),
            pltpu.VMEM((T, HALF), F32),
            blocks(2, 32),
            blocks(2, 8),
            blocks(2, 4, 4),
            blocks(2, 4, 2),
            blocks(2, 4),
            pltpu.VMEM((256, 256), F32),
            pieces(64),
            pieces(2, 32),
            pieces(4, 8),
            pieces(8),
            pieces(4),
            pieces(8),
            pieces(32),
            pieces(64),
            pltpu.SemaphoreType.DMA((9,)),
            pltpu.SemaphoreType.DMA((COPIES,)),
            pltpu.SemaphoreType.DMA((COPIES,)),
        ],
        compiler_params=pltpu.CompilerParams(
            collective_id=0, has_side_effects=True, vmem_limit_bytes=60 * 2**20
        ),
        cost_estimate=pl.CostEstimate(flops=5 * 10**9, bytes_accessed=6 * 2**20, transcendentals=2**17),
        name="layer",
    )(
        tile_count,
        tile_rows.reshape(1, T),
        tile_cols.reshape(1, T),
        features.reshape(4, T, 256),
        weight,
        cotangent.reshape(4, T, 256),
        tile_values.reshape(T, T, T),
    )
    hidden, grad_feat, grad_weight = pl.pallas_call(
        finish_kernel,
        out_shape=out_shape,
        in_specs=[hbm] * 3,
        out_specs=[vmem] * 3,
        scratch_shapes=[pltpu.SemaphoreType.DMA((3,))],
        name="finish",
    )(hidden, grad_feat, grad_weight)
    return hidden.reshape(4 * T, 256), grad_feat.reshape(4 * T, 256), grad_weight


def solution(mesh):
    placed = (
        P(("row", "col"), None),
        P(),
        P(("row", "col"), None),
        P("row", "col", None),
        P("row", "col", None),
        P("row", "col", None, None, None),
        P("row", "col"),
    )
    return jax.shard_map(
        per_device,
        mesh=mesh,
        in_specs=placed,
        out_specs=(P(("row", "col"), None), P(("row", "col"), None), P()),
        check_vma=False,
    )
```

```python
import functools

import jax
import jax.numpy as jnp
from jax import lax
from jax.experimental import pallas as pl
from jax.experimental.pallas import tpu as pltpu
from jax.sharding import PartitionSpec as P

MESH = pl.DeviceIdType.MESH
BF16 = jnp.bfloat16
F32 = jnp.float32
T = 128
HALF = 128
COPIES = 340
GROUP = 64
URGENT = (4, 3, 5, 2, 6, 1, 7, 0)


def position():
    row, col = lax.axis_index("row"), lax.axis_index("col")
    return dict(
        x_hi=col // 16, z=lax.rem(col // 2, 8), core=lax.rem(col, 2), y=row // 2, x_lo=lax.rem(row, 2)
    )


def device(here, x_hi=0, x_lo=0, y=0, z=0, core=0):
    x_hi = 1 - here["x_hi"] if x_hi else here["x_hi"]
    x_lo = 1 - here["x_lo"] if x_lo else here["x_lo"]
    core = 1 - here["core"] if core else here["core"]
    y = lax.rem(here["y"] + y, 4)
    z = lax.rem(here["z"] + z, 8)
    return (y * 2 + x_lo, x_hi * 16 + z * 2 + core)


ROW_TILE, ROW_KEEP, ROW_LAST, ROW_FEAT, COL_TILE, COL_KEEP, COL_LAST, COL_GRAD = range(8)
LINES = 16


def fill_table(here, count, rows, cols, table_ref):
    lane = lax.broadcasted_iota(jnp.int32, (T, T), 1)
    sub = lax.broadcasted_iota(jnp.int32, (T, T), 0)
    eye = lane == sub

    def spread(values):
        return jnp.broadcast_to(values, (T, T))

    def column(values):
        return jnp.broadcast_to(jnp.sum(jnp.where(eye, spread(values), 0), axis=1, keepdims=True), (T, T))

    def total(values):
        return jnp.sum(values, axis=0, keepdims=True)

    live_down = sub < count

    def feat_place(cols):
        owner = cols // 4
        return ((lax.rem(owner, 2) + here["x_lo"]) % 2 * 4 + (owner // 2 - here["y"] + 4) % 4) * 4 + lax.rem(cols, 4)

    def row_place(rows, order):
        owner, block = rows // 4, lax.rem(rows, 4)
        x_other = (owner // 16 + here["x_hi"]) % 2
        z_away = (lax.rem(owner // 2, 8) - here["z"] + 8) % 8
        core_other = (lax.rem(owner, 2) + here["core"]) % 2
        return (core_other * 8 + z_away) * 8 + order(block, x_other)

    def sum_order(block, x_other):
        return jnp.where(block < 2, 2 * block + x_other, 2 + block + 2 * x_other)

    def far_last(block, x_other):
        return block + 4 * x_other

    def far_first(block, x_other):
        return 2 * block + x_other

    rows_down, cols_down = column(rows), feat_place(column(cols))
    grads_down = [row_place(rows_down, far_last), row_place(rows_down, far_first)]
    rows_down = row_place(rows_down, sum_order)
    rows, cols = row_place(rows, sum_order), feat_place(cols)

    def sorted_by(keys, keys_down, values_down):
        big = T * T
        key = jnp.where(lane < count, spread(keys) * T + lane, big + lane)
        key_down = jnp.where(live_down, keys_down * T + sub, big + sub)
        rank_down = jnp.sum(jnp.where(key < key_down, 1, 0), axis=1, keepdims=True)
        rank_down = jnp.broadcast_to(rank_down, (T, T))
        now = rank_down == lane
        tile = total(jnp.where(now, sub, 0))
        values = [total(jnp.where(now, value, 0)) for value in values_down]
        mine = total(jnp.where(now, keys_down, 0))
        before = total(jnp.where(rank_down == lane - 1, keys_down, 0))
        first = lax.broadcasted_iota(jnp.int32, (1, T), 1) == 0
        keep = jnp.where(jnp.logical_or(first, mine != before), 0, 1)
        upto = total(jnp.where(jnp.logical_and(live_down, keys_down <= lane), 1, 0))
        some = total(jnp.where(jnp.logical_and(live_down, keys_down == lane), 1, 0))
        return [tile, keep, jnp.where(some > 0, upto - 1, T), *values]

    lines = sorted_by(rows, rows_down, [cols_down]) + sorted_by(cols, cols_down, grads_down)
    table_ref[...] = jnp.zeros_like(table_ref)
    for number, line in enumerate(lines):
        table_ref[number : number + 1, :] = line


def each(count, body):
    def step(i, carried):
        body(i)
        return carried

    lax.fori_loop(0, count, step, 0)


def add_up(out, terms):
    def body(i):
        rows = pl.ds(i * 32, 32)
        total = terms[0][:, rows].astype(F32)
        for term in terms[1:]:
            total = total + term[:, rows].astype(F32)
        out[:, rows] = total.astype(out.dtype)

    each(T // 32, body)


class Links:
    def __init__(self, send_sem, recv_sem):
        self.send_sem, self.recv_sem, self.copies = send_sem, recv_sem, []

    def send(self, src, dst, to):
        number = len(self.copies)
        copy = pltpu.make_async_remote_copy(
            src_ref=src,
            dst_ref=dst,
            send_sem=self.send_sem.at[number],
            recv_sem=self.recv_sem.at[number],
            device_id=to,
            device_id_type=MESH,
        )
        copy.start()
        self.copies.append(copy)
        return copy


def layer_kernel(
    count_hbm,
    rows_hbm,
    cols_hbm,
    feat_hbm,
    weight_hbm,
    cot_hbm,
    tile_hbm,
    hidden,
    grad_feat,
    grad_weight,
    table,
    lines,
    count,
    rows_in,
    cols_in,
    weight,
    tiles,
    cot,
    feats0,
    feats1,
    slots,
    give,
    core_in,
    value,
    x_in,
    ring_in,
    x_last,
    part,
    summed,
    grads0,
    grads1,
    carry,
    back,
    back_x,
    back_y,
    back_y2,
    back_x2,
    w_sum,
    w_own,
    w_core,
    w_y,
    w_z,
    w_x,
    w_all_z,
    w_all_y,
    w_all,
    local_sem,
    send_sem,
    recv_sem,
):
    here = position()
    feats, grads = (feats0, feats1), (grads0, grads1)
    links = Links(send_sem, recv_sem)
    z_up, z_down = device(here, z=1), device(here, z=7)
    x_far, x_near = device(here, x_hi=1), device(here, x_lo=1)
    x_both = device(here, x_hi=1, x_lo=1)
    twin = device(here, core=1)
    y_to = {d: device(here, y=d) for d in (1, 2, 3)}
    z_to = {d: device(here, z=d) for d in range(1, 8)}

    feat_own = [feat_hbm.at[:, :, pl.ds(f * HALF, HALF)] for f in range(2)]
    moves = [
        (rows_hbm, rows_in),
        (cols_hbm, cols_in),
        (feat_own[0], feats[0].at[pl.ds(0, 4)]),
        (feat_own[1], feats[1].at[pl.ds(0, 4)]),
        (tile_hbm, tiles),
        (weight_hbm, weight),
        (cot_hbm, cot),
        (count_hbm, count),
    ]
    loads = [pltpu.make_async_copy(src, dst, local_sem.at[i]) for i, (src, dst) in enumerate(moves)]
    for load in loads:
        load.start()

    barrier = pltpu.get_barrier_semaphore()
    partners = [x_far, x_near, twin, z_up, z_down, *y_to.values()]
    for partner in partners:
        pl.semaphore_signal(barrier, inc=1, device_id=partner, device_id_type=MESH)
    pl.semaphore_wait(barrier, len(partners))

    def over(f, src, place, size=2):
        return {d: links.send(src, feats[f].at[pl.ds((4 - d) * 4 + place, size)], y_to[d]) for d in (1, 3)}

    def relay(f, copies, place, size=1):
        sent = []
        for d, group, first in ((1, 12, 0), (3, 4, size)):
            copies[d].wait_recv()
            src = feats[f].at[pl.ds(group + place + first, size)]
            sent.append(links.send(src, feats[f].at[pl.ds(8 + place + first, size)], y_to[d]))
        return sent

    def across(f, group):
        rows = group * 4 + 2
        return links.send(feats[f].at[pl.ds(rows, 2)], feats[f].at[pl.ds(16 + rows, 2)], x_near)

    def gather_mixed():
        own = [feat_own[0].at[pl.ds(b, 2)] for b in (0, 2)]
        near = [links.send(own[0], feats[0].at[pl.ds(16, 2)], x_near)]
        late = over(0, own[1], 2)
        near.append(links.send(own[1], feats[0].at[pl.ds(18, 2)], x_near))
        return near, late, over(0, own[0], 0)

    def gather_rest(first):
        near, late, early = first
        late_two = relay(0, late, 2)
        copies = [near[1], across(0, 3), across(0, 1)]
        near[0].wait_recv()
        near_over = over(0, feats[0].at[pl.ds(16, 2)], 16)
        copies += relay(0, early, 0)
        for copy in late_two:
            copy.wait_recv()
        copies.append(across(0, 2))
        return copies + relay(0, near_over, 16)

    def gather_plain():
        own = feat_own[1]
        copies = [links.send(own, feats[1].at[pl.ds((4 - d) * 4, 4)], y_to[d]) for d in (2, 1, 3)]
        return links.send(own, feats[1].at[pl.ds(16, 4)], x_near), copies

    def gather_near(first):
        near, copies = first
        near.wait_recv()
        return copies + [
            links.send(feats[1].at[pl.ds(16, 4)], feats[1].at[pl.ds(16 + (4 - d) * 4, 4)], y_to[d])
            for d in (2, 1, 3)
        ]

    def products(f, piece, pieces, back_pass):
        tile_line, value_line, keep_line = (
            (COL_TILE, COL_GRAD + f, COL_KEEP) if back_pass else (ROW_TILE, ROW_FEAT, ROW_KEEP)
        )
        steps = T // GROUP // pieces
        source = (grads if back_pass else feats)[f]

        def step(i):
            total = carry[...]
            for u in range(GROUP):
                t = i * GROUP + u
                tile = tiles[table[tile_line, t]]
                block = source[table[value_line, t]]
                if back_pass:
                    tile = tile.T
                term = jnp.dot(tile, block, preferred_element_type=F32)
                total = term + total * table[keep_line, t].astype(F32)
                slots[f, t] = total.astype(BF16)
            carry[...] = total

        each(steps, lambda i: step(piece * steps + i))

    def core_send(f):
        copies = {}
        for dz in URGENT:

            def fill(place, dz=dz):
                give[f, dz * 8 + place] = slots[f, table[ROW_LAST, 64 + dz * 8 + place]]

            each(8, fill)
            span = pl.ds(dz * 8, 8)
            copies[dz] = links.send(give.at[f, span], core_in.at[f, span], twin)
        return copies

    def core_sum(f, dz, copies):
        copies[dz].wait_recv()

        def fill(place):
            at = dz * 8 + place
            own = slots[f, table[ROW_LAST, at]].astype(F32)
            value[f, at] = (own + core_in[f, at].astype(F32)).astype(BF16)

        each(8, fill)
        return links.send(value.at[f, pl.ds(dz * 8 + 6, 2)], x_in.at[f, pl.ds(dz * 2, 2)], x_far)

    class Ring:
        def __init__(self, f, stream, x_copies=None):
            self.f, self.stream, self.x_copies = f, stream, x_copies
            self.up = self.down = None

        def span(self, dz, first=0, size=2):
            return value.at[self.f, pl.ds(dz * 8 + self.stream * 2 + first, size)]

        def own(self, dz, first=0, size=2):
            if self.x_copies is None:
                return [self.span(dz, first, size)]
            return [self.span(dz, first, size), x_in.at[self.f, pl.ds(dz * 2 + first, size)]]

        def slot(self, way, step, first=0, size=2):
            return ring_in.at[self.f, self.stream, way, pl.ds(step * 2 + first, size)]

        def step(self, s):
            if s == 0:
                if self.x_copies is not None:
                    self.x_copies[4].wait_recv()
                    add_up(self.span(4), self.own(4))
                self.up = links.send(self.span(4, 0, 1), self.slot(0, 0, 0, 1), z_up)
                self.down = links.send(self.span(4, 1, 1), self.slot(1, 0, 1, 1), z_down)
                return
            for way, dz in ((0, 4 - s), (1, 4 + s)):
                if self.x_copies is not None:
                    self.x_copies[dz].wait_recv()
                (self.up, self.down)[way].wait_recv()
                if s == 1:
                    add_up(self.span(dz, way, 1), self.own(dz, way, 1) + [self.slot(way, 0, way, 1)])
                    if self.x_copies is not None:
                        add_up(self.span(dz, 1 - way, 1), self.own(dz, 1 - way, 1))
                else:
                    add_up(self.span(dz), self.own(dz) + [self.slot(way, s - 1)])
                sent = links.send(self.span(dz), self.slot(way, s), (z_up, z_down)[way])
                if way == 0:
                    self.up = sent
                else:
                    self.down = sent

        def finish(self):
            if self.x_copies is not None:
                self.x_copies[0].wait_recv()
            self.up.wait_recv()
            self.down.wait_recv()

        def last(self, first, size):
            return self.own(0, first, size) + [self.slot(0, 3, first, size), self.slot(1, 3, first, size)]

    def finish_z(f, b, ring):
        ring.finish()
        far = pl.ds(2 * f + b, 1)
        add_up(x_last.at[0, far], ring.last(1, 1))
        copy = links.send(x_last.at[0, far], x_last.at[1, far], x_far)
        add_up(part.at[f, pl.ds(b, 1)], ring.last(0, 1))
        return copy

    def close_z(f, b, copy):
        copy.wait_recv()
        add_up(
            summed.at[pl.ds(b, 1), :, pl.ds(f * HALF, HALF)],
            [part.at[f, pl.ds(b, 1)], x_last.at[1, pl.ds(2 * f + b, 1)]],
        )

    def close_x(f, ring):
        ring.finish()
        add_up(summed.at[pl.ds(2, 2), :, pl.ds(f * HALF, HALF)], ring.last(0, 2))

    def middle(pair):
        def body(i):
            b = 2 * pair + i
            rows = summed[b]
            pre = jnp.dot(rows, weight[...], preferred_element_type=F32)
            sig = jax.nn.sigmoid(pre)
            hidden[b] = (pre * sig).astype(BF16)
            grad_pre = (cot[b].astype(F32) * sig * (1.0 + pre * (1.0 - sig))).astype(BF16)
            own = lax.dot_general(
                grad_pre, weight[...], (((1,), (1,)), ((), ())), preferred_element_type=F32
            )
            grads[0][b] = own[:, :HALF].astype(BF16)
            grads[1][2 * b] = own[:, HALF:].astype(BF16)
            w_sum[...] += jnp.dot(rows.T, grad_pre, preferred_element_type=F32)

        each(2, body)

    first = gather_mixed()
    for load in (loads[0], loads[1], loads[7]):
        load.wait()
    fill_table(here, count[0, 0], rows_in[...], cols_in[...], lines)
    table_copy = pltpu.make_async_copy(lines, table, local_sem.at[8])
    table_copy.start()
    second = gather_rest(first)
    first1 = gather_plain()
    for load in loads[2:7]:
        load.wait()
    table_copy.wait()
    for f in range(2):
        slots[f, T] = jnp.zeros((T, HALF), BF16)
    w_sum[...] = jnp.zeros_like(w_sum)
    carry[...] = jnp.zeros_like(carry)
    for copy in second:
        copy.wait_recv()
    products(0, 0, 1, False)
    core0 = core_send(0)
    second1 = gather_near(first1)
    x0, x1, last = {}, {}, {}
    z0 = [Ring(0, 0), Ring(0, 1)]
    z1 = [Ring(1, 0), Ring(1, 1)]
    ring_x0, ring_x1 = Ring(0, 2, x0), Ring(1, 2, x1)

    def step_all(rings, s):
        for ring in rings:
            ring.step(s)

    for dz in URGENT:
        x0[dz] = core_sum(0, dz, core0)
        if dz == 4:
            step_all(z0, 0)
    step_all(z0, 1)
    ring_x0.step(0)
    for copy in second1:
        copy.wait_recv()
    products(1, 0, 2, False)
    step_all(z0, 2)
    products(1, 1, 2, False)
    core1 = core_send(1)
    step_all(z0, 3)
    ring_x0.step(1)
    for dz in URGENT:
        x1[dz] = core_sum(1, dz, core1)
        if dz == 4:
            step_all(z1, 0)
    ring_x0.step(2)
    step_all(z1, 1)
    ring_x1.step(0)
    for b in range(2):
        last[0, b] = finish_z(0, b, z0[b])
    ring_x0.step(3)
    step_all(z1, 2)
    ring_x1.step(1)
    for b in range(2):
        close_z(0, b, last[0, b])
    step_all(z1, 3)
    ring_x1.step(2)
    close_x(0, ring_x0)
    for b in range(2):
        last[1, b] = finish_z(1, b, z1[b])
    ring_x1.step(3)
    for b in range(2):
        close_z(1, b, last[1, b])
    middle(0)

    class Spread:
        def __init__(self, f, place):
            self.f, self.place = f, place
            self.up = self.down = None

        def span(self, dz, first=0, size=2):
            return grads[self.f].at[pl.ds((dz % 8) * 8 + self.place + first, size)]

        def step(self, s):
            if s > 0:
                self.done()
            first, size = ((0, 2), (1, 1))[s == 3]
            self.up = links.send(self.span(-s, 0, size), self.span(-s - 1, 0, size), z_up)
            self.down = links.send(self.span(s, first, size), self.span(s + 1, first, size), z_down)

        def done(self):
            self.up.wait_recv()
            self.down.wait_recv()

    from_twin = {0: [], 1: []}
    from_far = {}

    def to_twin(f, dz, place, size):
        at = dz * 8 + place
        from_twin[f].append(links.send(grads[f].at[pl.ds(at, size)], grads[f].at[pl.ds(64 + at, size)], twin))

    def to_far(dz, place):
        at = dz * 8 + place
        from_far[dz, place] = links.send(grads[0].at[pl.ds(at, 2)], grads[0].at[pl.ds(at + 4, 2)], x_far)

    def near(b):
        return links.send(grads[1].at[pl.ds(2 * b, 1)], grads[1].at[pl.ds(2 * b + 1, 1)], x_far)

    def around(s):
        return sorted({-s % 8, s % 8})

    late = [Spread(0, 0), Spread(0, 2)]
    early = [Spread(1, 2 * b) for b in range(4)]

    def late_round(s):
        for stream in late:
            if s < 4:
                stream.step(s)
            else:
                stream.done()
            for dz in around(s):
                to_far(dz, stream.place)
        for dz in around(s):
            to_twin(0, dz, 0, 4)

    def early_round(s):
        for b, stream in enumerate(early):
            if s == 0:
                nears[b].wait_recv()
            if s < 4:
                stream.step(s)
            else:
                stream.done()
            if b % 2:
                for dz in around(s):
                    to_twin(1, dz, 4 * (b // 2), 4)

    def far_to_twin(s):
        for dz in around(s):
            for place in (0, 2):
                from_far[dz, place].wait_recv()
            to_twin(0, dz, 4, 4)

    def all_here(f):
        for copy in from_twin[f]:
            copy.wait_recv()

    nears = [near(0), near(1)]
    late[0].step(0)
    to_far(0, 0)
    close_x(1, ring_x1)
    middle(1)
    nears += [near(2), near(3)]
    late[1].step(0)
    to_far(0, 2)
    to_twin(0, 0, 0, 4)

    def weight_start():
        def fill(i):
            for j in range(2):
                w_own[2 * i + j] = w_sum[pl.ds(8 * i, 8), j * 128 : (j + 1) * 128]

        each(32, fill)
        return links.send(w_own.at[pl.ds((1 - here["core"]) * 32, 32)], w_core.at[0], twin)

    def weight_y(copy):
        copy.wait_recv()

        def fill(i):
            w_core[1, i] = w_own[here["core"] * 32 + i] + w_core[0, i]

        each(32, fill)
        return [
            links.send(w_core.at[1, pl.ds(lax.rem(here["y"] + d, 4) * 8, 8)], w_y.at[d], y_to[d]) for d in (1, 2, 3)
        ]

    def weight_z(copies):
        for copy in copies:
            copy.wait_recv()

        def fill(i):
            w_y[0, i] = w_core[1, here["y"] * 8 + i] + w_y[1, i] + w_y[2, i] + w_y[3, i]

        each(8, fill)
        return [
            links.send(w_y.at[0, pl.ds(lax.rem(here["z"] + d, 8), 1)], w_z.at[pl.ds(d, 1)], z_to[d])
            for d in range(1, 8)
        ]

    def weight_x(copies):
        for copy in copies:
            copy.wait_recv()
        total = w_y[0, pl.ds(here["z"], 1)]
        for d in range(1, 8):
            total = total + w_z[d : d + 1]
        w_x[0:1] = total
        return [
            links.send(w_x.at[pl.ds(0, 1)], w_x.at[pl.ds(i, 1)], to)
            for i, to in ((1, x_far), (2, x_near), (3, x_both))
        ]

    def weight_all_z(copies):
        for copy in copies:
            copy.wait_recv()
        mine = pl.ds(here["z"], 1)
        w_all_z[mine] = (w_x[0:1] + w_x[1:2]) + (w_x[2:3] + w_x[3:4])
        return [links.send(w_all_z.at[mine], w_all_z.at[mine], z_to[d]) for d in range(1, 8)]

    def weight_all_y(copies):
        for copy in copies:
            copy.wait_recv()
        mine = pl.ds(here["y"] * 8, 8)

        def fill(i):
            w_all_y[here["y"] * 8 + i] = w_all_z[i]

        each(8, fill)
        return [links.send(w_all_y.at[mine], w_all_y.at[mine], y_to[d]) for d in (1, 2, 3)]

    def weight_all_core(copies):
        for copy in copies:
            copy.wait_recv()
        mine = pl.ds(here["core"] * 32, 32)

        def fill(i):
            w_all[here["core"] * 32 + i] = w_all_y[i]

        each(32, fill)
        return links.send(w_all.at[mine], w_all.at[mine], twin)

    def weight_end(copy):
        copy.wait_recv()

        def fill(i):
            for j in range(2):
                grad_weight[pl.ds(8 * i, 8), j * 128 : (j + 1) * 128] = w_all[2 * i + j]

        each(32, fill)

    def back_first(f):
        def fill(place):
            back[f, place] = slots[f, table[COL_LAST, place]]

        each(32, fill)
        near_copies = {
            d: links.send(back.at[f, pl.ds((4 + d) * 4, 2)], back_x.at[f, pl.ds(d * 2, 2)], x_near)
            for d in (2, 1, 3, 0)
        }
        y_copies = [
            links.send(back.at[f, pl.ds((x_other * 4 + d) * 4 + 2, 2)], back_y.at[f, d, pl.ds(x_other * 2, 2)], y_to[d])
            for x_other in (1, 0)
            for d in (2, 1, 3)
        ]
        return near_copies, y_copies

    def back_second(f, first):
        near_copies, y_copies = first
        y_second = []
        for d in (2, 1, 3, 0):
            near_copies[d].wait_recv()
            own = back.at[f, pl.ds(d * 4, 2)]
            add_up(own, [own, back_x.at[f, pl.ds(d * 2, 2)]])
            if d:
                y_second.append(links.send(back.at[f, pl.ds(d * 4, 2)], back_y2.at[f, d], y_to[d]))
        for copy in y_copies[:3]:
            copy.wait_recv()
        add_up(
            back_x2.at[f, pl.ds(0, 2)],
            [back.at[f, pl.ds(18, 2)]] + [back_y.at[f, d, pl.ds(2, 2)] for d in (1, 2, 3)],
        )
        near_second = links.send(back_x2.at[f, pl.ds(0, 2)], back_x2.at[f, pl.ds(2, 2)], x_near)
        return y_copies[3:], y_second, near_second

    def back_third(f, second):
        y_copies, y_second, near_second = second
        lanes = pl.ds(f * HALF, HALF)
        for copy in y_copies + [near_second]:
            copy.wait_recv()
        add_up(
            grad_feat.at[pl.ds(2, 2), :, lanes],
            [back.at[f, pl.ds(2, 2)], back_x2.at[f, pl.ds(2, 2)]]
            + [back_y.at[f, d, pl.ds(0, 2)] for d in (1, 2, 3)],
        )
        for copy in y_second:
            copy.wait_recv()
        add_up(
            grad_feat.at[pl.ds(0, 2), :, lanes],
            [back.at[f, pl.ds(0, 2)]] + [back_y2.at[f, d] for d in (1, 2, 3)],
        )

    w_copy = weight_start()
    late_round(1)
    early_round(0)
    w_copy = weight_y(w_copy)
    late_round(2)
    early_round(1)
    late_round(3)
    w_copy = weight_z(w_copy)
    far_to_twin(0)
    far_to_twin(1)
    early_round(2)
    late_round(4)
    w_copy = weight_x(w_copy)
    far_to_twin(2)
    early_round(3)
    w_copy = weight_all_z(w_copy)
    far_to_twin(3)
    far_to_twin(4)
    early_round(4)
    all_here(0)
    products(0, 0, 1, True)
    first0 = back_first(0)
    w_copy = weight_all_y(w_copy)
    all_here(1)
    products(1, 0, 2, True)
    second0 = back_second(0, first0)
    products(1, 1, 2, True)
    first1 = back_first(1)
    w_copy = weight_all_core(w_copy)
    back_third(0, second0)
    second1 = back_second(1, first1)
    weight_end(w_copy)
    back_third(1, second1)
    for copy in links.copies:
        copy.wait_send()


def finish_kernel(*refs):
    copies = [pltpu.make_async_copy(refs[i], refs[3 + i], refs[6].at[i]) for i in range(3)]
    for copy in copies:
        copy.start()
    for copy in copies:
        copy.wait()


def per_device(features, weight, cotangent, tile_rows, tile_cols, tile_values, tile_count):
    hbm, vmem = pl.BlockSpec(memory_space=pl.ANY), pl.BlockSpec(memory_space=pltpu.VMEM)

    def blocks(*counts):
        return pltpu.VMEM((*counts, T, HALF), BF16)

    def pieces(*counts):
        return pltpu.VMEM((*counts, 8, 128), F32)

    out_shape = (
        jax.ShapeDtypeStruct((4, T, 256), BF16),
        jax.ShapeDtypeStruct((4, T, 256), BF16),
        jax.ShapeDtypeStruct((256, 256), F32),
    )
    hidden, grad_feat, grad_weight = pl.pallas_call(
        layer_kernel,
        out_shape=out_shape,
        in_specs=[hbm] * 7,
        out_specs=(vmem, vmem, vmem),
        scratch_shapes=[
            pltpu.SMEM((LINES, T), jnp.int32),
            pltpu.VMEM((LINES, T), jnp.int32),
            pltpu.SMEM((1, 1), jnp.int32),
            pltpu.VMEM((1, T), jnp.int32),
            pltpu.VMEM((1, T), jnp.int32),
            pltpu.VMEM((256, 256), BF16),
            blocks(T),
            pltpu.VMEM((4, T, 256), BF16),
            blocks(32),
            blocks(32),
            blocks(2, T + 1),
            blocks(2, 64),
            blocks(2, 64),
            blocks(2, 64),
            blocks(2, 16),
            blocks(2, 3, 2, 8),
            blocks(2, 4),
            pltpu.VMEM((2, 2, T, HALF), F32),
            pltpu.VMEM((4, T, 256), BF16),
            blocks(128),
            blocks(128),
            pltpu.VMEM((T, HALF), F32),
            blocks(2, 32),
            blocks(2, 8),
            blocks(2, 4, 4),
            blocks(2, 4, 2),
            blocks(2, 4),
            pltpu.VMEM((256, 256), F32),
            pieces(64),
            pieces(2, 32),
            pieces(4, 8),
            pieces(8),
            pieces(4),
            pieces(8),
            pieces(32),
            pieces(64),
            pltpu.SemaphoreType.DMA((9,)),
            pltpu.SemaphoreType.DMA((COPIES,)),
            pltpu.SemaphoreType.DMA((COPIES,)),
        ],
        compiler_params=pltpu.CompilerParams(
            collective_id=0, has_side_effects=True, vmem_limit_bytes=60 * 2**20
        ),
        cost_estimate=pl.CostEstimate(flops=5 * 10**9, bytes_accessed=6 * 2**20, transcendentals=2**17),
        name="layer",
    )(
        tile_count,
        tile_rows.reshape(1, T),
        tile_cols.reshape(1, T),
        features.reshape(4, T, 256),
        weight,
        cotangent.reshape(4, T, 256),
        tile_values.reshape(T, T, T),
    )
    hidden, grad_feat, grad_weight = pl.pallas_call(
        finish_kernel,
        out_shape=out_shape,
        in_specs=[hbm] * 3,
        out_specs=[vmem] * 3,
        scratch_shapes=[pltpu.SemaphoreType.DMA((3,))],
        name="finish",
    )(hidden, grad_feat, grad_weight)
    return hidden.reshape(4 * T, 256), grad_feat.reshape(4 * T, 256), grad_weight


def solution(mesh):
    placed = (
        P(("row", "col"), None),
        P(),
        P(("row", "col"), None),
        P("row", "col", None),
        P("row", "col", None),
        P("row", "col", None, None, None),
        P("row", "col"),
    )
    return jax.shard_map(
        per_device,
        mesh=mesh,
        in_specs=placed,
        out_specs=(P(("row", "col"), None), P(("row", "col"), None), P()),
        check_vma=False,
    )
```
